32 devices in a mesh: cand: 8 (over z, y), tp: 4 (over x, core).
Axes of the slice: x: 2, y: 2, z: 4, core: 2. Of those that a mesh axis runs over, the one named last changes fastest.
Arguments:
- reward_query: bfloat16 [64, 32, 8192], P('cand', None, 'tp'), may hold values from -170 to 170
- reward_new: bfloat16 [64, 2, 32, 1024], P('cand', None, None, 'tp'), may hold values from -7 to 7
- reward_key_value_cache: bfloat16 [64, 2, 768, 1024], P('cand', None, None, 'tp'), may hold values from -6 to 6
- reward_length: int32 [64], P('cand'), may hold values from 1 to 768
- out_weight: bfloat16 [8192, 4096], P('tp'), may hold values from -0.09375 to 0.09375
- policy_cache: bfloat16 [64, 2, 768, 1024], P('cand', None, None, 'tp'), may hold values from -6 to 6
- policy_length: int32 [64], replicated, may hold values from 1 to 767
- source: int32 [32], replicated, may hold values from 0 to 63, as said below
- policy_query: bfloat16 [32, 8192], P('cand', 'tp'), may hold values from -170 to 170
- policy_new: bfloat16 [32, 2, 1024], P('cand', None, 'tp'), may hold values from -7 to 7
Outputs:
- reward_out: bfloat16 [2048, 4096], P('cand', 'tp')
- compacted: bfloat16 [32, 2, 768, 1024], P('cand', None, None, 'tp')
- policy_attn: bfloat16 [32, 8192], P('cand', 'tp')
The draws below stay inside these ranges and needn't reach their ends.
Inputs may be any that keep to these rules, and one draw needn't show every extreme that they name: `source`: distinct candidate indices; the 8 candidates of each index of cand are named exactly 4 times.
All inputs are finite; a program needn't handle non-finite values.
Results may differ from the reference program's by a relative error of at most 0.0057.
Values may be sent and summed in bfloat16 or wider, within the bound.
No kernel may reach another device: no remote copies, remote signals or barrier semaphores. Data moves between devices by JAX's collectives and lax.ppermute only.
A program may use at most 128 MiB of HBM per device.

```python
import jax
import jax.numpy as jnp
from jax import lax

ASKING_UNITS = 64
SHARED_KV_UNITS = 8
ATTN_DIM = 128
DOUT = 4096
NEW_TOKEN_COUNT = 32
CACHE_LENGTH = 768
CPG = 8
SLOT_DEV = 4
CANDIDATE_COUNT = 64
RETAINED_TOTAL = 32


def truncated_gaussian(key, tag, shape):
    return jnp.clip(jax.random.normal(jax.random.fold_in(key, tag), shape, jnp.float32), -6.0, 6.0)


def prefix_entries(key):
    return truncated_gaussian(key, 42, (CANDIDATE_COUNT, SHARED_KV_UNITS * ATTN_DIM))


def chosen_parents(key):
    group_count = CANDIDATE_COUNT // CPG
    group_keys = jax.random.split(jax.random.fold_in(key, 51), group_count)
    orders = jax.vmap(lambda one_key: jax.random.permutation(one_key, CPG))(group_keys)
    retained_entries = orders[:, :SLOT_DEV] + (jnp.arange(group_count, dtype=jnp.int32) * CPG)[:, None]
    retained_entries = retained_entries.reshape(RETAINED_TOTAL).astype(jnp.int32)
    return jax.random.permutation(jax.random.fold_in(key, 52), retained_entries).astype(jnp.int32)


def draw_reward_new(key, part):
    appended_symbols = truncated_gaussian(key, 31, (CANDIDATE_COUNT, 2, NEW_TOKEN_COUNT, SHARED_KV_UNITS * ATTN_DIM))
    return appended_symbols.astype(jnp.bfloat16)


def draw_reward_query(key, part):
    probe_entries = truncated_gaussian(key, 32, (CANDIDATE_COUNT, NEW_TOKEN_COUNT, ASKING_UNITS * ATTN_DIM))
    return probe_entries.astype(jnp.bfloat16)


def draw_reward_length(key, part):
    drawn = jax.random.randint(jax.random.fold_in(key, 61), (CANDIDATE_COUNT,), 1, CACHE_LENGTH + 1)
    marked = jax.random.randint(jax.random.fold_in(key, 62), (), 0, CANDIDATE_COUNT)
    return jnp.where(jnp.arange(CANDIDATE_COUNT) == marked, CACHE_LENGTH, drawn).astype(jnp.int32)


def draw_policy_length(key, part):
    drawn = jax.random.randint(jax.random.fold_in(key, 63), (CANDIDATE_COUNT,), 1, CACHE_LENGTH)
    marked = jax.random.randint(jax.random.fold_in(key, 64), (), 0, CANDIDATE_COUNT)
    return jnp.where(jnp.arange(CANDIDATE_COUNT) == marked, CACHE_LENGTH - 1, drawn).astype(jnp.int32)


def draw_source(key, part):
    return chosen_parents(key)


def draw_policy_cache(key, part):
    layer_cache = truncated_gaussian(key, 41, (CANDIDATE_COUNT, 2, CACHE_LENGTH, SHARED_KV_UNITS * ATTN_DIM))
    layer_cache = layer_cache.at[:, 0, 0, :].set(prefix_entries(key))
    return layer_cache.astype(jnp.bfloat16)


def draw_policy_query(key, part):
    probe_entries = truncated_gaussian(key, 43, (RETAINED_TOTAL, ASKING_UNITS * ATTN_DIM))
    return probe_entries.astype(jnp.bfloat16)


def draw_policy_new(key, part):
    appended_symbols = truncated_gaussian(key, 44, (RETAINED_TOTAL, 2, SHARED_KV_UNITS * ATTN_DIM))
    return appended_symbols.astype(jnp.bfloat16)


def with_spikes(entries, rng, source, target, parts, factor):
    def block_of(axis_at):
        return (jnp.arange(entries.shape[axis_at]) // (entries.shape[axis_at] // parts)).reshape((-1,) + (1,) * (entries.ndim - 1 - axis_at))

    one_side = jax.random.permutation(rng, parts)[block_of(target)]
    far = (block_of(target) + parts // 2) % parts
    return jnp.where((block_of(source) == one_side) | (block_of(source) == far), factor * entries, entries)


def steps_of(stream_key, dims, pieces, low, largest):
    factor_of, own = 1.0, jax.random.fold_in(stream_key, 6)
    for axis_at, parts in pieces:
        heights = jnp.exp(jax.random.uniform(jax.random.fold_in(own, axis_at), (parts,), jnp.float32, low / len(pieces), largest / len(pieces)))
        factor_of = factor_of * jnp.repeat(heights, dims[axis_at] // parts).reshape([-1 if axis == axis_at else 1 for axis in range(len(dims))])
    return factor_of


def gaussian(key, extent, width, bound, cuts=(), kind=jnp.bfloat16):
    values = width * jax.random.normal(key, extent, jnp.float32)
    if cuts:
        values = values * steps_of(key, extent, cuts, -0.22, 0.18)
    return jnp.clip(values, -bound, bound).astype(kind)


def heavy_noise(stream_key, dims, deviation, limit, cuts, heavy, held_as=jnp.bfloat16):
    entries = deviation * jax.random.normal(stream_key, dims, jnp.float32)
    if cuts:
        entries = entries * steps_of(stream_key, dims, cuts, -0.22, 0.18)
    return jnp.clip(with_spikes(entries, jax.random.fold_in(stream_key, 3), *heavy), -limit, limit).astype(held_as)


def setup_inputs(seed: int = 0) -> dict:
    key_of = jax.random.split(jax.random.key(seed), 11)
    return {
        "reward_query": draw_reward_query(jax.random.fold_in(key_of[10], 71), 0),
        "reward_new": draw_reward_new(jax.random.fold_in(key_of[10], 71), 0),
        "reward_key_value_cache": gaussian(key_of[2], (CANDIDATE_COUNT, 2, CACHE_LENGTH, SHARED_KV_UNITS * ATTN_DIM), 1.0, 6.0, ((0, 8), (3, 4))),
        "reward_length": draw_reward_length(jax.random.fold_in(key_of[10], 71), 0),
        "out_weight": heavy_noise(key_of[4], (ASKING_UNITS * ATTN_DIM, DOUT), (ASKING_UNITS * ATTN_DIM) ** -0.5, 0.09375, ((0, 4),), (0, 1, 4, 2.0)),
        "policy_cache": draw_policy_cache(jax.random.fold_in(key_of[10], 71), 0),
        "policy_length": draw_policy_length(jax.random.fold_in(key_of[10], 71), 0),
        "source": draw_source(jax.random.fold_in(key_of[10], 71), 0),
        "policy_query": draw_policy_query(jax.random.fold_in(key_of[10], 71), 0),
        "policy_new": draw_policy_new(jax.random.fold_in(key_of[10], 71), 0),
    }


def reward_one(inputs):
    probe_entries, new_key_value, layer_cache, length = inputs
    attention_clusters = ASKING_UNITS // SHARED_KV_UNITS
    key_rows = jnp.concatenate([layer_cache[0], new_key_value[0]], axis=0).astype(jnp.float32).reshape(CACHE_LENGTH + NEW_TOKEN_COUNT, SHARED_KV_UNITS, ATTN_DIM)
    value_rows = jnp.concatenate([layer_cache[1], new_key_value[1]], axis=0).astype(jnp.float32).reshape(CACHE_LENGTH + NEW_TOKEN_COUNT, SHARED_KV_UNITS, ATTN_DIM)
    head_list = probe_entries.astype(jnp.float32).reshape(NEW_TOKEN_COUNT, SHARED_KV_UNITS, attention_clusters, ATTN_DIM)
    scores = jnp.einsum("tkgd,pkd->kgtp", head_list, key_rows) * (ATTN_DIM ** -0.5)
    position = jnp.arange(CACHE_LENGTH + NEW_TOKEN_COUNT, dtype=jnp.int32)
    token = jnp.arange(NEW_TOKEN_COUNT, dtype=jnp.int32)
    visible = (position[None, :] < length) | ((position[None, :] >= CACHE_LENGTH) & (position[None, :] - CACHE_LENGTH <= token[:, None]))
    scores = jnp.where(visible, scores, -1e30)
    weights = jax.nn.softmax(scores, axis=-1).astype(jnp.bfloat16)
    mixed = jnp.einsum("kgtp,pkd->tkgd", weights.astype(jnp.float32), value_rows)
    return mixed.reshape(NEW_TOKEN_COUNT, ASKING_UNITS * ATTN_DIM).astype(jnp.bfloat16)


def policy_one(inputs):
    probe_entries, layer_cache, length = inputs
    attention_clusters = ASKING_UNITS // SHARED_KV_UNITS
    key_rows = layer_cache[0].astype(jnp.float32).reshape(CACHE_LENGTH, SHARED_KV_UNITS, ATTN_DIM)
    value_rows = layer_cache[1].astype(jnp.float32).reshape(CACHE_LENGTH, SHARED_KV_UNITS, ATTN_DIM)
    head_list = probe_entries.astype(jnp.float32).reshape(SHARED_KV_UNITS, attention_clusters, ATTN_DIM)
    scores = jnp.einsum("kgd,pkd->kgp", head_list, key_rows) * (ATTN_DIM ** -0.5)
    position = jnp.arange(CACHE_LENGTH, dtype=jnp.int32)
    scores = jnp.where(position <= length, scores, -1e30)
    weights = jax.nn.softmax(scores, axis=-1).astype(jnp.bfloat16)
    mixed = jnp.einsum("kgp,pkd->kgd", weights.astype(jnp.float32), value_rows)
    return mixed.reshape(ASKING_UNITS * ATTN_DIM).astype(jnp.bfloat16)


def reference(reward_query, reward_new, reward_key_value_cache, reward_length, out_weight, policy_cache, policy_length, source, policy_query, policy_new):
    attn_rows = lax.map(reward_one, (reward_query, reward_new, reward_key_value_cache, reward_length))
    attn_rows = attn_rows.reshape(CANDIDATE_COUNT * NEW_TOKEN_COUNT, ASKING_UNITS * ATTN_DIM)
    reward_out = jnp.dot(attn_rows, out_weight, preferred_element_type=jnp.float32).astype(jnp.bfloat16)
    moved = policy_cache[source]
    slot_lengths = policy_length[source].astype(jnp.int32)
    position = jnp.arange(CACHE_LENGTH, dtype=jnp.int32)
    compacted = jnp.where(position[None, None, :, None] == slot_lengths[:, None, None, None], policy_new[:, :, None, :], moved)
    policy_attn = lax.map(policy_one, (policy_query, compacted, slot_lengths))
    return reward_out, compacted, policy_attn
```

```python
import jax
import jax.numpy as jnp
from jax import lax
from jax.sharding import PartitionSpec as P

ASKING_UNITS = 64
SHARED_KV_UNITS = 8
ATTN_DIM = 128
NEW_TOKEN_COUNT = 32
CACHE_LENGTH = 768


def body(
    reward_query,
    reward_new,
    reward_key_value_cache,
    reward_length,
    out_weight,
    policy_cache,
    policy_length,
    source,
    policy_query,
    policy_new,
):
    attention_clusters = ASKING_UNITS // SHARED_KV_UNITS
    score_scale = ATTN_DIM ** (-0.5)
    count = reward_query.shape[0]
    kv_heads = reward_key_value_cache.shape[-1] // ATTN_DIM
    head_list = reward_query.reshape(count, NEW_TOKEN_COUNT, kv_heads, attention_clusters, ATTN_DIM)
    cache_keys = reward_key_value_cache[:, 0].reshape(count, CACHE_LENGTH, kv_heads, ATTN_DIM)
    cache_values = reward_key_value_cache[:, 1].reshape(count, CACHE_LENGTH, kv_heads, ATTN_DIM)
    fresh_keys = reward_new[:, 0].reshape(count, NEW_TOKEN_COUNT, kv_heads, ATTN_DIM)
    fresh_values = reward_new[:, 1].reshape(count, NEW_TOKEN_COUNT, kv_heads, ATTN_DIM)
    old_scores = (
        jnp.einsum("ctkgd,cpkd->ckgtp", head_list, cache_keys, preferred_element_type=jnp.float32)
        * score_scale
    )
    new_scores = (
        jnp.einsum("ctkgd,cukd->ckgtu", head_list, fresh_keys, preferred_element_type=jnp.float32)
        * score_scale
    )
    cache_rows = lax.iota(jnp.int32, CACHE_LENGTH)
    old_visible = cache_rows[None, :] < reward_length[:, None]
    old_scores = jnp.where(old_visible[:, None, None, None, :], old_scores, -1e30)
    token_rows = lax.iota(jnp.int32, NEW_TOKEN_COUNT)
    new_visible = token_rows[None, :] <= token_rows[:, None]
    new_scores = jnp.where(new_visible, new_scores, -1e30)
    peak = jnp.maximum(old_scores.max(-1), new_scores.max(-1))[..., None]
    old_exp = jnp.exp(old_scores - peak)
    new_exp = jnp.exp(new_scores - peak)
    denominator = old_exp.sum(-1, keepdims=True) + new_exp.sum(-1, keepdims=True)
    old_weights = (old_exp / denominator).astype(jnp.bfloat16)
    new_weights = (new_exp / denominator).astype(jnp.bfloat16)
    mixed = jnp.einsum(
        "ckgtp,cpkd->ctkgd", old_weights, cache_values, preferred_element_type=jnp.float32
    )
    mixed = mixed + jnp.einsum(
        "ckgtu,cukd->ctkgd", new_weights, fresh_values, preferred_element_type=jnp.float32
    )
    attn_rows = mixed.reshape(
        count * NEW_TOKEN_COUNT, kv_heads * attention_clusters * ATTN_DIM
    ).astype(jnp.bfloat16)
    partial_value = jnp.dot(attn_rows, out_weight, preferred_element_type=jnp.float32)
    reward_out = lax.psum_scatter(partial_value, "tp", scatter_dimension=1, tiled=True).astype(
        jnp.bfloat16
    )
    slot_count = policy_query.shape[0]
    per_index = policy_cache.shape[0]
    owner = source // per_index
    slots = lax.iota(jnp.int32, source.shape[0])
    earlier = (owner[:, None] == owner[None, :]) & (slots[None, :] < slots[:, None])
    rank = jnp.sum(earlier.astype(jnp.int32), axis=1)
    me = lax.axis_index("cand")
    lane = lax.iota(jnp.int32, slot_count)
    mine = (owner[None, :] == me) & (rank[None, :] == lane[:, None])
    named = jnp.sum(jnp.where(mine, source[None, :] - me * per_index, 0), axis=1)
    picked = jnp.take(policy_cache, named, axis=0)
    spread = lax.all_to_all(picked, "cand", split_axis=2, concat_axis=0, tiled=True)
    selected = jnp.take(spread, owner * slot_count + rank, axis=0)
    moved = lax.all_to_all(selected, "cand", split_axis=0, concat_axis=2, tiled=True)
    local_source = lax.dynamic_slice_in_dim(source, lax.axis_index("cand") * slot_count, slot_count)
    slot_lengths = jnp.take(policy_length, local_source)
    compacted = jnp.where(
        cache_rows[None, None, :, None] == slot_lengths[:, None, None, None],
        policy_new[:, :, None, :],
        moved,
    )
    slot_heads = policy_query.reshape(slot_count, kv_heads, attention_clusters, ATTN_DIM)
    slot_keys = compacted[:, 0].reshape(slot_count, CACHE_LENGTH, kv_heads, ATTN_DIM)
    slot_values = compacted[:, 1].reshape(slot_count, CACHE_LENGTH, kv_heads, ATTN_DIM)
    slot_scores = (
        jnp.einsum("skgd,spkd->skgp", slot_heads, slot_keys, preferred_element_type=jnp.float32)
        * score_scale
    )
    slot_visible = cache_rows[None, :] <= slot_lengths[:, None]
    slot_scores = jnp.where(slot_visible[:, None, None, :], slot_scores, -1e30)
    slot_weights = jax.nn.softmax(slot_scores, axis=-1).astype(jnp.bfloat16)
    policy_attn = jnp.einsum(
        "skgp,spkd->skgd", slot_weights, slot_values, preferred_element_type=jnp.float32
    )
    policy_attn = policy_attn.reshape(slot_count, kv_heads * attention_clusters * ATTN_DIM).astype(
        jnp.bfloat16
    )
    return (reward_out, compacted, policy_attn)


def solution(mesh):
    in_specs = (
        P("cand", None, "tp"),
        P("cand", None, None, "tp"),
        P("cand", None, None, "tp"),
        P("cand"),
        P("tp", None),
        P("cand", None, None, "tp"),
        P(),
        P(),
        P("cand", "tp"),
        P("cand", None, "tp"),
    )
    out_specs = (P("cand", "tp"), P("cand", None, None, "tp"), P("cand", "tp"))
    return jax.shard_map(body, mesh=mesh, in_specs=in_specs, out_specs=out_specs, check_vma=False)
```

```python
import functools

import jax
import jax.numpy as jnp
from jax import lax
from jax.experimental import pallas as pl
from jax.experimental.pallas import tpu as pltpu
from jax.sharding import PartitionSpec as P

ASKING_UNITS = 64
SHARED_KV_UNITS = 8
ATTN_DIM = 128
NEW_TOKEN_COUNT = 32
CACHE_LENGTH = 768

GRID_Z = 4
GRID_Y = 2
GRID = GRID_Z * GRID_Y
ROUNDS = [(2, 1)] + [(1, 2)] * 8
LAST = len(ROUNDS) - 1
PLACE = [3 * sum(many for many, _ in ROUNDS[:turn]) for turn in range(len(ROUNDS) + 1)]
SENT = PLACE[-1]
NEXT = 2 * SENT
LOG = 128
SLOTS = 4 * GRID
UP = [(n, n + 2) for n in range(6)]
DOWN = [(n + 2, n) for n in range(6)]
ACROSS = [(n, n + 1 - 2 * (n % 2)) for n in range(8)]

VMEM_GRANT = 60 * 1024 * 1024
LOG2_E = 1.4426950408889634

ANY = pl.BlockSpec(memory_space=pl.ANY)
HBM = pl.BlockSpec(memory_space=pltpu.HBM)
SMEM = pl.BlockSpec(memory_space=pltpu.SMEM)
VMEM = pl.BlockSpec(memory_space=pltpu.VMEM)
LITTLE = pl.CostEstimate(flops=1000, bytes_accessed=1000, transcendentals=0)


def choose(state, many, lag, open_all=False):
    z, y, wait, last_z, last_y, lane_y = state
    me = lax.axis_index("cand")
    need_z = z != last_z
    next_y = jnp.where(need_z, lane_y, last_y)
    move_y = y != next_y
    move = jnp.where(move_y, 2, jnp.where(need_z, jnp.where(last_z > z, 0, 1), 3))
    after = jnp.where(need_z & (lane_y != last_y), 1, 0)
    steps = jnp.abs(z - last_z) + jnp.where(move_y, 1, 0) + after
    left = jnp.sum(jnp.where(move < 3, 1.0, 0.0)).astype(jnp.int32)
    ready = move < 3
    if not open_all:
        ready = ready & (wait <= 0)
    link = jnp.where(ready, move * GRID + z * GRID_Y + y, 99)
    column = lax.broadcasted_iota(jnp.int32, (1, 128), 1)
    key = (steps * 128 + 127 - column).astype(jnp.float32)
    rows = lax.broadcasted_iota(jnp.int32, (3 * GRID, 128), 0)
    names = (lax.broadcasted_iota(jnp.int32, (3 * GRID, 128), 1) + 1).astype(jnp.float32)
    keys = jnp.where(rows == link, key, -1.0)
    partner = me + 1 - 2 * lax.rem(me, 2)
    out_scale = (
        jnp.where(rows == me, 1.0, 0.0)
        + jnp.where(rows == me + GRID, 128.0, 0.0)
        + jnp.where(rows == me + 2 * GRID, 16384.0, 0.0)
    )
    in_scale = (
        jnp.where(rows == me - 2, 1.0, 0.0)
        + jnp.where((rows == me + 2 + GRID) & (rows < 2 * GRID), 128.0, 0.0)
        + jnp.where(rows == partner + 2 * GRID, 16384.0, 0.0)
    )
    moved = jnp.zeros_like(key)
    sent, got = [], []
    for _ in range(many):
        best = jnp.max(keys, axis=1, keepdims=True)
        won = (keys == best) & (keys >= 0.0)
        number = jnp.where(won, names, 0.0)
        keys = jnp.where(won, -1.0, keys)
        moved = jnp.maximum(moved, jnp.max(number, axis=0, keepdims=True))
        for packed, into in ((jnp.sum(number * out_scale), sent), (jnp.sum(number * in_scale), got)):
            packed = packed.astype(jnp.int32)
            into += [packed & 127, (packed >> 7) & 127, packed >> 14]
    moved = moved > 0.0
    z = jnp.where(moved, z + jnp.where(move == 0, 1, 0) - jnp.where(move == 1, 1, 0), z)
    y = jnp.where(moved & (move == 2), 1 - y, y)
    wait = jnp.where(moved, lag - 1, jnp.maximum(wait - 1, 0))
    return [z, y, wait, last_z, last_y, lane_y], sent, got, left


def parcel_from(number, source_ref, log_ref, cache_ref, arrivals, held_ref, target, sem):
    index = number - 1
    slot, half = index >> 1, index & 1
    per_index = cache_ref.shape[0]
    local = source_ref[jnp.maximum(slot, 0)] - lax.axis_index("cand") * per_index
    own = (number > 0) & (local >= 0) & (local < per_index)
    elsewhere = (number > 0) & jnp.logical_not(own)

    @pl.when(own)
    def _():
        pltpu.make_async_copy(cache_ref.at[local, half], target, sem).start()

    for i, ref in enumerate(arrivals):
        match = elsewhere & (log_ref[i] == number)
        if held_ref is not None:
            elsewhere = elsewhere & (log_ref[i] != number)

        @pl.when(match)
        def _(ref=ref):
            pltpu.make_async_copy(ref, target, sem).start()

    if held_ref is not None:

        @pl.when(elsewhere)
        def _():
            pltpu.make_async_copy(held_ref.at[index], target, sem).start()


def each_parcel(arrivals):
    parcels = []
    for first in range(0, len(arrivals), 3):
        triple = arrivals[first : first + 3]
        parcels += [ref.at[i] for i in range(triple[0].shape[0]) for ref in triple]
    return parcels


def lay_out(numbers, source_ref, log_ref, cache_ref, arrivals, sends, room, in_sem, out_sem):
    many = sends[0].shape[0]

    def put(i):
        return pltpu.make_async_copy(room.at[i], sends[i % 3].at[i // 3], out_sem.at[i])

    def begin():
        for i in range(3 * many):
            parcel_from(numbers[i], source_ref, log_ref, cache_ref, arrivals, None, room.at[i], in_sem.at[i])

    def end():
        for i in range(3 * many):

            @pl.when(numbers[i] > 0)
            def _(i=i):
                pltpu.make_async_copy(cache_ref.at[0, 0], room.at[i], in_sem.at[i]).wait()
                put(i).start()

        for i in range(3 * many):

            @pl.when(numbers[i] > 0)
            def _(i=i):
                put(i).wait()

    return begin, end


def lay_out_scratch(many, cache):
    return [
        pltpu.VMEM((3 * many,) + cache.shape[2:], cache.dtype),
        pltpu.SemaphoreType.DMA((3 * many,)),
        pltpu.SemaphoreType.DMA((3 * many,)),
    ]


def sends_of(many, cache):
    return [jax.ShapeDtypeStruct((many,) + cache.shape[2:], cache.dtype)] * 3


def first_kernel(source_ref, cache_ref, log_out, state_out, up, down, across, *scratch):
    parcel = lax.broadcasted_iota(jnp.int32, (1, 128), 1)
    owner = jnp.zeros_like(parcel)
    for i in range(SLOTS):
        owner = jnp.where((parcel >> 1) == i, source_ref[i] >> 3, owner)
    target = jnp.where(parcel < 2 * SLOTS, parcel >> 3, 0)
    state = [owner >> 1, owner & 1, jnp.zeros_like(parcel), target >> 1, target & 1, parcel & 1]
    state, sent, got, _ = choose(state, *ROUNDS[0])
    begin, end = lay_out(sent, source_ref, None, cache_ref, [], (up, down, across), *scratch)
    begin()
    for i in range(LOG):
        log_out[i] = 0
    for i in range(len(got)):
        log_out[i] = got[i]
        log_out[SENT + i] = sent[i]
    for i in range(6):
        state_out[i : i + 1, :] = state[i]
    end()


def first_stage(source, cache):
    many, _ = ROUNDS[0]
    log, state, *sends = pl.pallas_call(
        first_kernel,
        out_shape=[jax.ShapeDtypeStruct((LOG,), jnp.int32), jax.ShapeDtypeStruct((8, 128), jnp.int32)]
        + sends_of(many, cache),
        in_specs=[SMEM, HBM],
        out_specs=[SMEM, VMEM, HBM, HBM, HBM],
        scratch_shapes=lay_out_scratch(many, cache),
        compiler_params=pltpu.CompilerParams(vmem_limit_bytes=VMEM_GRANT),
        cost_estimate=LITTLE,
    )(source, cache)
    return log, state, sends


def plan_kernel(log_ref, state_ref, log_out, state_out, left_out):
    state = [state_ref[i : i + 1, :] for i in range(6)]
    for i in range(LOG):
        log_out[i] = log_ref[i]
    for turn in range(1, len(ROUNDS)):
        state, sent, got, _ = choose(state, *ROUNDS[turn])
        for i in range(len(got)):
            log_out[PLACE[turn] + i] = got[i]
            log_out[SENT + PLACE[turn] + i] = sent[i]
    state, sent, got, left = choose(state, 1, 1, True)
    for i in range(3):
        log_out[NEXT + i] = sent[i]
        log_out[NEXT + 3 + i] = got[i]
    left_out[0] = left
    for i in range(6):
        state_out[i : i + 1, :] = state[i]


def plan(log, state):
    return pl.pallas_call(
        plan_kernel,
        out_shape=[
            jax.ShapeDtypeStruct(log.shape, jnp.int32),
            jax.ShapeDtypeStruct(state.shape, jnp.int32),
            jax.ShapeDtypeStruct((1,), jnp.int32),
        ],
        in_specs=[SMEM, VMEM],
        out_specs=[SMEM, VMEM, SMEM],
        cost_estimate=LITTLE,
    )(log, state)


def stage_kernel(turn, count, source_ref, log_ref, cache_ref, *refs):
    arrivals = each_parcel(refs[:count])
    sends = refs[count : count + 3]
    many, _ = ROUNDS[turn]
    sent = [log_ref[SENT + PLACE[turn] + i] for i in range(3 * many)]
    begin, end = lay_out(sent, source_ref, log_ref, cache_ref, arrivals, sends, *refs[count + 3 :])
    begin()
    end()


def stage(source, log, cache, arrivals, turn):
    many, _ = ROUNDS[turn]
    return pl.pallas_call(
        functools.partial(stage_kernel, turn, len(arrivals)),
        out_shape=sends_of(many, cache),
        in_specs=[SMEM, SMEM, HBM] + [ANY] * len(arrivals),
        out_specs=[HBM] * 3,
        scratch_shapes=lay_out_scratch(many, cache),
        compiler_params=pltpu.CompilerParams(vmem_limit_bytes=VMEM_GRANT),
        cost_estimate=LITTLE,
    )(source, log, cache, *arrivals)


def late_kernel(count, source_ref, log_ref, state_ref, cache_ref, *refs):
    arrivals = each_parcel(refs[:count])
    held_in, log_out, state_out, left_out, up, down, across, held_out, store_sem, send_sem = refs[count:]
    sends = (up, down, across)
    latest = arrivals[-3:]
    place = PLACE[LAST]
    number = [log_ref[place + i] for i in range(3)]
    for i, ref in enumerate(latest):

        @pl.when(number[i] > 0)
        def _(i=i, ref=ref):
            pltpu.make_async_copy(ref, held_out.at[number[i] - 1], store_sem.at[i]).start()

    sent = [log_ref[NEXT + i] for i in range(3)]
    for i in range(3):
        parcel_from(
            sent[i], source_ref, log_ref, cache_ref, arrivals, held_in, sends[i].at[0], send_sem.at[i]
        )
    state, next_sent, next_got, left = choose([state_ref[i : i + 1, :] for i in range(6)], 1, 1, True)
    for i in range(place):
        log_out[i] = log_ref[i]
    for i in range(3):
        log_out[place + i] = log_ref[NEXT + 3 + i]
        log_out[NEXT + i] = next_sent[i]
        log_out[NEXT + 3 + i] = next_got[i]
    left_out[0] = left
    for i in range(6):
        state_out[i : i + 1, :] = state[i]
    for i in range(3):

        @pl.when(sent[i] > 0)
        def _(i=i):
            pltpu.make_async_copy(cache_ref.at[0, 0], sends[i].at[0], send_sem.at[i]).wait()

    for i, ref in enumerate(latest):

        @pl.when(number[i] > 0)
        def _(i=i, ref=ref):
            pltpu.make_async_copy(ref, held_out.at[number[i] - 1], store_sem.at[i]).wait()


def late_stage(source, log, state, cache, arrivals, held):
    count = len(arrivals)
    out = pl.pallas_call(
        functools.partial(late_kernel, count),
        out_shape=[
            jax.ShapeDtypeStruct((LOG,), jnp.int32),
            jax.ShapeDtypeStruct((8, 128), jnp.int32),
            jax.ShapeDtypeStruct((1,), jnp.int32),
        ]
        + sends_of(1, cache)
        + [jax.ShapeDtypeStruct(held.shape, held.dtype)],
        in_specs=[SMEM, SMEM, VMEM, HBM] + [ANY] * (count - 3) + [VMEM] * 3 + [HBM],
        out_specs=[SMEM, VMEM, SMEM, VMEM, VMEM, VMEM, HBM],
        scratch_shapes=[pltpu.SemaphoreType.DMA((3,)), pltpu.SemaphoreType.DMA((3,))],
        input_output_aliases={4 + count: 6},
        cost_estimate=LITTLE,
    )(source, log, state, cache, *arrivals, held)
    log, state, left, *rest = out
    return log, state, left, rest[:3], rest[3]


def room_kernel(out_ref):
    pass


def room(parcels, cache):
    return pl.pallas_call(
        room_kernel,
        out_shape=jax.ShapeDtypeStruct((parcels,) + cache.shape[2:], cache.dtype),
        out_specs=HBM,
        cost_estimate=LITTLE,
    )()


def exchange(sends):
    up, down, across = sends
    return (
        lax.ppermute(up, "cand", UP),
        lax.ppermute(down, "cand", DOWN),
        lax.ppermute(across, "cand", ACROSS),
    )


def slot_attention(q_rows, keys, values, length, score_scale):
    scores = lax.dot_general(q_rows, keys, (((1,), (1,)), ((), ())), preferred_element_type=jnp.float32)
    scores = scores * score_scale
    position = lax.broadcasted_iota(jnp.int32, scores.shape, 1)
    scores = jnp.where(position <= length, scores, -1e30)
    weights = jnp.exp(scores - jnp.max(scores, axis=1, keepdims=True))
    total = jnp.sum(weights, axis=1, keepdims=True)
    mixed = jnp.dot(weights.astype(jnp.bfloat16), values, preferred_element_type=jnp.float32)
    return mixed / total


def finish_kernel(count, *refs):
    source_ref, length_ref, log_ref, query_ref, new_ref, cache_ref = refs[:6]
    arrivals = each_parcel(refs[6 : 6 + count])
    held_ref, compacted_ref, attn_ref, rows, attn, sem, out_sem = refs[6 + count :]
    me = lax.axis_index("cand")
    slots, _, depth, width = rows.shape
    kv_heads = width // ATTN_DIM
    group = query_ref.shape[1] // width
    for s in range(slots):
        for half in range(2):
            number = (me * slots + s) * 2 + half + 1
            parcel_from(
                number, source_ref, log_ref, cache_ref, arrivals, held_ref, rows.at[s, half], sem.at[2 * s + half]
            )
    query = query_ref[...].astype(jnp.float32)
    for s in range(slots):
        length = length_ref[source_ref[me * slots + s]]
        base = pl.multiple_of((length >> 4) << 4, 16)
        for half in range(2):
            pltpu.make_async_copy(cache_ref.at[0, 0], rows.at[s, half], sem.at[2 * s + half]).wait()
            window = rows[s, half, pl.ds(base, 16), :]
            row = lax.broadcasted_iota(jnp.int32, window.shape, 0)
            fresh_row = new_ref[s, half : half + 1, :]
            rows[s, half, pl.ds(base, 16), :] = jnp.where(
                row == length - base, fresh_row.astype(jnp.float32), window.astype(jnp.float32)
            ).astype(window.dtype)
            pltpu.make_async_copy(rows.at[s, half], compacted_ref.at[s, half], out_sem.at[2 * s + half]).start()
        for k in range(kv_heads):
            columns = slice(k * ATTN_DIM, (k + 1) * ATTN_DIM)
            heads = [slice((k * group + g) * ATTN_DIM, (k * group + g + 1) * ATTN_DIM) for g in range(group)]
            mixed = slot_attention(
                jnp.concatenate([query[s : s + 1, h] for h in heads], axis=0).astype(query_ref.dtype),
                rows[s, 0, :, columns],
                rows[s, 1, :, columns],
                length,
                ATTN_DIM ** (-0.5),
            )
            for g, h in enumerate(heads):
                attn[s : s + 1, h] = mixed[g : g + 1, :]
    attn_ref[...] = attn[...].astype(attn_ref.dtype)
    for s in range(slots):
        for half in range(2):
            pltpu.make_async_copy(rows.at[s, half], compacted_ref.at[s, half], out_sem.at[2 * s + half]).wait()


def finish(source, policy_length, log, query, new, cache, arrivals, held):
    slots = query.shape[0]
    _, _, depth, width = cache.shape
    return pl.pallas_call(
        functools.partial(finish_kernel, len(arrivals)),
        out_shape=[
            jax.ShapeDtypeStruct((slots, 2, depth, width), cache.dtype),
            jax.ShapeDtypeStruct(query.shape, query.dtype),
        ],
        in_specs=[SMEM, SMEM, SMEM, VMEM, VMEM, HBM] + [ANY] * len(arrivals) + [HBM],
        out_specs=[HBM, VMEM],
        scratch_shapes=[
            pltpu.VMEM((slots, 2, depth, width), cache.dtype),
            pltpu.VMEM(query.shape, jnp.float32),
            pltpu.SemaphoreType.DMA((2 * slots,)),
            pltpu.SemaphoreType.DMA((2 * slots,)),
        ],
        compiler_params=pltpu.CompilerParams(vmem_limit_bytes=VMEM_GRANT),
        cost_estimate=LITTLE,
    )(source, policy_length, log, query, new, cache, *arrivals, held)


def routed_policy(policy_cache, policy_length, source, policy_query, policy_new, reward_inputs):
    first_log, first_state, sends = first_stage(source, policy_cache)
    arrivals = list(exchange(sends))
    log, state, left = plan(first_log, first_state)
    log, *reward_inputs = lax.optimization_barrier((log, *reward_inputs))
    share = reward_share(*reward_inputs)
    log, share = lax.optimization_barrier((log, share))
    for turn in range(1, len(ROUNDS)):
        at_hand = arrivals[: 3 * sum(sent + lag <= turn for sent, (_, lag) in enumerate(ROUNDS[:turn]))]
        sends = stage(source, log, policy_cache, at_hand, turn)
        log, *sends = lax.optimization_barrier((log, *sends))
        arrivals += exchange(sends)
        if turn == 1:
            log, share = lax.optimization_barrier((log, share))
            reward_out = add_shares(share)
    early, latest = arrivals[:-3], arrivals[-3:]
    left, reward_out = lax.optimization_barrier((left, reward_out))

    def unfinished(carry):
        return carry[0][0] > 0

    def one_round(carry):
        _, log, state, latest, held = carry
        log, state, left, sends, held = late_stage(source, log, state, policy_cache, early + latest, held)
        return left, log, state, list(exchange(sends)), held

    held = room(2 * SLOTS, policy_cache)
    _, log, _, latest, held = lax.while_loop(unfinished, one_round, (left, log, state, latest, held))
    compacted, attn = finish(
        source, policy_length, log, policy_query, policy_new, policy_cache, early + latest, held
    )
    return reward_out, compacted, attn


def spread_policy(policy_cache, policy_length, source, policy_query, policy_new, reward_inputs):
    reward_out = add_shares(reward_share(*reward_inputs))
    attention_clusters = ASKING_UNITS // SHARED_KV_UNITS
    score_scale = ATTN_DIM ** (-0.5)
    kv_heads = policy_cache.shape[-1] // ATTN_DIM
    cache_rows = lax.iota(jnp.int32, CACHE_LENGTH)
    slot_count = policy_query.shape[0]
    per_index = policy_cache.shape[0]
    owner = source // per_index
    slots = lax.iota(jnp.int32, source.shape[0])
    earlier = (owner[:, None] == owner[None, :]) & (slots[None, :] < slots[:, None])
    rank = jnp.sum(earlier.astype(jnp.int32), axis=1)
    me = lax.axis_index("cand")
    lane = lax.iota(jnp.int32, slot_count)
    mine = (owner[None, :] == me) & (rank[None, :] == lane[:, None])
    named = jnp.sum(jnp.where(mine, source[None, :] - me * per_index, 0), axis=1)
    picked = jnp.take(policy_cache, named, axis=0)
    spread = lax.all_to_all(picked, "cand", split_axis=2, concat_axis=0, tiled=True)
    selected = jnp.take(spread, owner * slot_count + rank, axis=0)
    moved = lax.all_to_all(selected, "cand", split_axis=0, concat_axis=2, tiled=True)
    local_source = lax.dynamic_slice_in_dim(source, lax.axis_index("cand") * slot_count, slot_count)
    slot_lengths = jnp.take(policy_length, local_source)
    compacted = jnp.where(
        cache_rows[None, None, :, None] == slot_lengths[:, None, None, None],
        policy_new[:, :, None, :],
        moved,
    )
    slot_heads = policy_query.reshape(slot_count, kv_heads, attention_clusters, ATTN_DIM)
    slot_keys = compacted[:, 0].reshape(slot_count, CACHE_LENGTH, kv_heads, ATTN_DIM)
    slot_values = compacted[:, 1].reshape(slot_count, CACHE_LENGTH, kv_heads, ATTN_DIM)
    slot_scores = (
        jnp.einsum("skgd,spkd->skgp", slot_heads, slot_keys, preferred_element_type=jnp.float32)
        * score_scale
    )
    slot_visible = cache_rows[None, :] <= slot_lengths[:, None]
    slot_scores = jnp.where(slot_visible[:, None, None, :], slot_scores, -1e30)
    slot_weights = jax.nn.softmax(slot_scores, axis=-1).astype(jnp.bfloat16)
    policy_attn = jnp.einsum(
        "skgp,spkd->skgd", slot_weights, slot_values, preferred_element_type=jnp.float32
    )
    policy_attn = policy_attn.reshape(slot_count, kv_heads * attention_clusters * ATTN_DIM).astype(
        jnp.bfloat16
    )
    return reward_out, compacted, policy_attn


def reward_kernel(
    length_ref, query_ref, new_ref, cache_ref, weight_ref, out_ref, query, new, cache, weight, rows, out, sem, weight_sem,
    out_sem,
):
    candidates, tokens, units = query.shape
    depth, width = cache.shape[2:]
    kv_heads = width // ATTN_DIM
    group = units // width
    blocks, _, block = weight.shape
    scale = ATTN_DIM ** (-0.5) * LOG2_E
    token = lax.rem(lax.broadcasted_iota(jnp.int32, (group * tokens, tokens), 0), tokens)
    new_visible = lax.broadcasted_iota(jnp.int32, (group * tokens, tokens), 1) <= token
    by_rows = (((1,), (1,)), ((), ()))

    def inputs(i):
        return [
            pltpu.make_async_copy(query_ref.at[i], query.at[i], sem.at[4 * i]),
            pltpu.make_async_copy(cache_ref.at[i, 0], cache.at[i, 0], sem.at[4 * i + 1]),
            pltpu.make_async_copy(new_ref.at[i], new.at[i], sem.at[4 * i + 2]),
            pltpu.make_async_copy(cache_ref.at[i, 1], cache.at[i, 1], sem.at[4 * i + 3]),
        ]

    def fetch(j):
        return pltpu.make_async_copy(weight_ref.at[:, pl.ds(j * block, block)], weight.at[j], weight_sem.at[j])

    def put(j):
        return pltpu.make_async_copy(out.at[j % 2], out_ref.at[:, pl.ds(j * block, block)], out_sem.at[j % 2])

    for i in range(min(3, candidates)):
        for copy in inputs(i):
            copy.start()
    fetched = 0
    for i in range(candidates):
        for copy in inputs(i):
            copy.wait()
        if i + 3 < candidates:
            for copy in inputs(i + 3):
                copy.start()
        while fetched < blocks * (i + 1) // candidates:
            fetch(fetched).start()
            fetched += 1
        visible = lax.broadcasted_iota(jnp.int32, (1, depth), 1) < length_ref[i]
        for k in range(kv_heads):
            columns = slice(k * ATTN_DIM, (k + 1) * ATTN_DIM)
            heads = [slice((k * group + g) * ATTN_DIM, (k * group + g + 1) * ATTN_DIM) for g in range(group)]
            asked = jnp.concatenate([query[i, :, h] for h in heads], axis=0)
            old = lax.dot_general(asked, cache[i, 0, :, columns], by_rows, preferred_element_type=jnp.float32)
            fresh = lax.dot_general(asked, new[i, 0, :, columns], by_rows, preferred_element_type=jnp.float32)
            old = jnp.where(visible, old, -1e30)
            fresh = jnp.where(new_visible, fresh, -1e30)
            peak = jnp.maximum(jnp.max(old, axis=1, keepdims=True), jnp.max(fresh, axis=1, keepdims=True))
            old = jnp.exp2((old - peak) * scale)
            fresh = jnp.exp2((fresh - peak) * scale)
            total = jnp.sum(old, axis=1, keepdims=True) + jnp.sum(fresh, axis=1, keepdims=True)
            mixed = jnp.dot(old.astype(jnp.bfloat16), cache[i, 1, :, columns], preferred_element_type=jnp.float32)
            mixed += jnp.dot(fresh.astype(jnp.bfloat16), new[i, 1, :, columns], preferred_element_type=jnp.float32)
            mixed = (mixed / total).astype(rows.dtype)
            for g, h in enumerate(heads):
                rows[i * tokens : (i + 1) * tokens, h] = mixed[g * tokens : (g + 1) * tokens, :]
    for j in range(blocks):
        fetch(j).wait()
        if j >= 2:
            put(j - 2).wait()
        out[j % 2] = jnp.dot(rows[...], weight[j], preferred_element_type=jnp.float32)
        put(j).start()
    put(blocks - 2).wait()
    put(blocks - 1).wait()


def reward_share(query, new, cache, length, weight):
    candidates, tokens, units = query.shape
    features = weight.shape[1]
    block = 512
    return pl.pallas_call(
        reward_kernel,
        out_shape=jax.ShapeDtypeStruct((candidates * tokens, features), jnp.float32),
        in_specs=[SMEM, HBM, HBM, HBM, HBM],
        out_specs=HBM,
        scratch_shapes=[
            pltpu.VMEM(query.shape, query.dtype),
            pltpu.VMEM(new.shape, new.dtype),
            pltpu.VMEM(cache.shape, cache.dtype),
            pltpu.VMEM((features // block, units, block), weight.dtype),
            pltpu.VMEM((candidates * tokens, units), query.dtype),
            pltpu.VMEM((2, candidates * tokens, block), jnp.float32),
            pltpu.SemaphoreType.DMA((4 * candidates,)),
            pltpu.SemaphoreType.DMA((features // block,)),
            pltpu.SemaphoreType.DMA((2,)),
        ],
        compiler_params=pltpu.CompilerParams(vmem_limit_bytes=VMEM_GRANT),
        cost_estimate=LITTLE,
    )(length, query, new, cache, weight)


def add_shares(share):
    return lax.psum_scatter(share, "tp", scatter_dimension=1, tiled=True).astype(jnp.bfloat16)


def body(
    cand_count,
    reward_query,
    reward_new,
    reward_key_value_cache,
    reward_length,
    out_weight,
    policy_cache,
    policy_length,
    source,
    policy_query,
    policy_new,
):
    policy = spread_policy
    if cand_count == GRID and policy_cache.shape[0] == 8 and source.shape[0] == SLOTS:
        policy = routed_policy
    reward_inputs = (reward_query, reward_new, reward_key_value_cache, reward_length, out_weight)
    return policy(policy_cache, policy_length, source, policy_query, policy_new, reward_inputs)


def solution(mesh):
    in_specs = (
        P("cand", None, "tp"),
        P("cand", None, None, "tp"),
        P("cand", None, None, "tp"),
        P("cand"),
        P("tp", None),
        P("cand", None, None, "tp"),
        P(),
        P(),
        P("cand", "tp"),
        P("cand", None, "tp"),
    )
    out_specs = (P("cand", "tp"), P("cand", None, None, "tp"), P("cand", "tp"))
    return jax.shard_map(
        functools.partial(body, mesh.shape["cand"]),
        mesh=mesh,
        in_specs=in_specs,
        out_specs=out_specs,
        check_vma=False,
    )
```

```python
import functools

import jax
import jax.numpy as jnp
from jax import lax
from jax.experimental import pallas as pl
from jax.experimental.pallas import tpu as pltpu
from jax.sharding import PartitionSpec as P

ASKING_UNITS = 64
SHARED_KV_UNITS = 8
ATTN_DIM = 128
NEW_TOKEN_COUNT = 32
CACHE_LENGTH = 768

GRID_Z = 4
GRID_Y = 2
GRID = GRID_Z * GRID_Y
ROUNDS = [(2, 1)] + [(1, 2)] * 8
LAST = len(ROUNDS) - 1
PLACE = [3 * sum(many for many, _ in ROUNDS[:turn]) for turn in range(len(ROUNDS) + 1)]
SENT = PLACE[-1]
NEXT = 2 * SENT
LOG = 128
SLOTS = 4 * GRID
UP = [(n, n + 2) for n in range(6)]
DOWN = [(n + 2, n) for n in range(6)]
ACROSS = [(n, n + 1 - 2 * (n % 2)) for n in range(8)]

VMEM_GRANT = 60 * 1024 * 1024
LOG2_E = 1.4426950408889634

ANY = pl.BlockSpec(memory_space=pl.ANY)
HBM = pl.BlockSpec(memory_space=pltpu.HBM)
SMEM = pl.BlockSpec(memory_space=pltpu.SMEM)
VMEM = pl.BlockSpec(memory_space=pltpu.VMEM)
LITTLE = pl.CostEstimate(flops=1000, bytes_accessed=1000, transcendentals=0)


def choose(state, many, lag, open_all=False):
    z, y, wait, last_z, last_y, lane_y = state
    me = lax.axis_index("cand")
    need_z = z != last_z
    next_y = jnp.where(need_z, lane_y, last_y)
    move_y = y != next_y
    move = jnp.where(move_y, 2, jnp.where(need_z, jnp.where(last_z > z, 0, 1), 3))
    after = jnp.where(need_z & (lane_y != last_y), 1, 0)
    steps = jnp.abs(z - last_z) + jnp.where(move_y, 1, 0) + after
    left = jnp.sum(jnp.where(move < 3, 1.0, 0.0)).astype(jnp.int32)
    ready = move < 3
    if not open_all:
        ready = ready & (wait <= 0)
    link = jnp.where(ready, move * GRID + z * GRID_Y + y, 99)
    column = lax.broadcasted_iota(jnp.int32, (1, 128), 1)
    key = (steps * 128 + 127 - column).astype(jnp.float32)
    rows = lax.broadcasted_iota(jnp.int32, (3 * GRID, 128), 0)
    names = (lax.broadcasted_iota(jnp.int32, (3 * GRID, 128), 1) + 1).astype(jnp.float32)
    keys = jnp.where(rows == link, key, -1.0)
    partner = me + 1 - 2 * lax.rem(me, 2)
    out_scale = (
        jnp.where(rows == me, 1.0, 0.0)
        + jnp.where(rows == me + GRID, 128.0, 0.0)
        + jnp.where(rows == me + 2 * GRID, 16384.0, 0.0)
    )
    in_scale = (
        jnp.where(rows == me - 2, 1.0, 0.0)
        + jnp.where((rows == me + 2 + GRID) & (rows < 2 * GRID), 128.0, 0.0)
        + jnp.where(rows == partner + 2 * GRID, 16384.0, 0.0)
    )
    moved = jnp.zeros_like(key)
    sent, got = [], []
    for _ in range(many):
        best = jnp.max(keys, axis=1, keepdims=True)
        won = (keys == best) & (keys >= 0.0)
        number = jnp.where(won, names, 0.0)
        keys = jnp.where(won, -1.0, keys)
        moved = jnp.maximum(moved, jnp.max(number, axis=0, keepdims=True))
        for packed, into in ((jnp.sum(number * out_scale), sent), (jnp.sum(number * in_scale), got)):
            packed = packed.astype(jnp.int32)
            into += [packed & 127, (packed >> 7) & 127, packed >> 14]
    moved = moved > 0.0
    z = jnp.where(moved, z + jnp.where(move == 0, 1, 0) - jnp.where(move == 1, 1, 0), z)
    y = jnp.where(moved & (move == 2), 1 - y, y)
    wait = jnp.where(moved, lag - 1, jnp.maximum(wait - 1, 0))
    return [z, y, wait, last_z, last_y, lane_y], sent, got, left


def parcel_from(number, source_ref, log_ref, cache_ref, arrivals, held_ref, target, sem):
    index = number - 1
    slot, half = index >> 1, index & 1
    per_index = cache_ref.shape[0]
    local = source_ref[jnp.maximum(slot, 0)] - lax.axis_index("cand") * per_index
    own = (number > 0) & (local >= 0) & (local < per_index)
    elsewhere = (number > 0) & jnp.logical_not(own)

    @pl.when(own)
    def _():
        pltpu.make_async_copy(cache_ref.at[local, half], target, sem).start()

    for i, ref in enumerate(arrivals):
        match = elsewhere & (log_ref[i] == number)
        if held_ref is not None:
            elsewhere = elsewhere & (log_ref[i] != number)

        @pl.when(match)
        def _(ref=ref):
            pltpu.make_async_copy(ref, target, sem).start()

    if held_ref is not None:

        @pl.when(elsewhere)
        def _():
            pltpu.make_async_copy(held_ref.at[index], target, sem).start()


def each_parcel(arrivals):
    parcels = []
    for first in range(0, len(arrivals), 3):
        triple = arrivals[first : first + 3]
        parcels += [ref.at[i] for i in range(triple[0].shape[0]) for ref in triple]
    return parcels


def lay_out(numbers, source_ref, log_ref, cache_ref, arrivals, sends, room, in_sem, out_sem):
    many = sends[0].shape[0]

    def put(i):
        return pltpu.make_async_copy(room.at[i], sends[i % 3].at[i // 3], out_sem.at[i])

    def begin():
        for i in range(3 * many):
            parcel_from(numbers[i], source_ref, log_ref, cache_ref, arrivals, None, room.at[i], in_sem.at[i])

    def end():
        for i in range(3 * many):

            @pl.when(numbers[i] > 0)
            def _(i=i):
                pltpu.make_async_copy(cache_ref.at[0, 0], room.at[i], in_sem.at[i]).wait()
                put(i).start()

        for i in range(3 * many):

            @pl.when(numbers[i] > 0)
            def _(i=i):
                put(i).wait()

    return begin, end


def lay_out_scratch(many, cache):
    return [
        pltpu.VMEM((3 * many,) + cache.shape[2:], cache.dtype),
        pltpu.SemaphoreType.DMA((3 * many,)),
        pltpu.SemaphoreType.DMA((3 * many,)),
    ]


def sends_of(many, cache):
    return [jax.ShapeDtypeStruct((many,) + cache.shape[2:], cache.dtype)] * 3


def first_kernel(source_ref, cache_ref, log_out, state_out, up, down, across, *scratch):
    parcel = lax.broadcasted_iota(jnp.int32, (1, 128), 1)
    owner = jnp.zeros_like(parcel)
    for i in range(SLOTS):
        owner = jnp.where((parcel >> 1) == i, source_ref[i] >> 3, owner)
    target = jnp.where(parcel < 2 * SLOTS, parcel >> 3, 0)
    state = [owner >> 1, owner & 1, jnp.zeros_like(parcel), target >> 1, target & 1, parcel & 1]
    state, sent, got, _ = choose(state, *ROUNDS[0])
    begin, end = lay_out(sent, source_ref, None, cache_ref, [], (up, down, across), *scratch)
    begin()
    for i in range(LOG):
        log_out[i] = 0
    for i in range(len(got)):
        log_out[i] = got[i]
        log_out[SENT + i] = sent[i]
    for i in range(6):
        state_out[i : i + 1, :] = state[i]
    end()


def first_stage(source, cache):
    many, _ = ROUNDS[0]
    log, state, *sends = pl.pallas_call(
        first_kernel,
        out_shape=[jax.ShapeDtypeStruct((LOG,), jnp.int32), jax.ShapeDtypeStruct((8, 128), jnp.int32)]
        + sends_of(many, cache),
        in_specs=[SMEM, HBM],
        out_specs=[SMEM, VMEM, HBM, HBM, HBM],
        scratch_shapes=lay_out_scratch(many, cache),
        compiler_params=pltpu.CompilerParams(vmem_limit_bytes=VMEM_GRANT),
        cost_estimate=LITTLE,
    )(source, cache)
    return log, state, sends


def plan_kernel(log_ref, state_ref, log_out, state_out, left_out):
    state = [state_ref[i : i + 1, :] for i in range(6)]
    for i in range(LOG):
        log_out[i] = log_ref[i]
    for turn in range(1, len(ROUNDS)):
        state, sent, got, _ = choose(state, *ROUNDS[turn])
        for i in range(len(got)):
            log_out[PLACE[turn] + i] = got[i]
            log_out[SENT + PLACE[turn] + i] = sent[i]
    state, sent, got, left = choose(state, 1, 1, True)
    for i in range(3):
        log_out[NEXT + i] = sent[i]
        log_out[NEXT + 3 + i] = got[i]
    left_out[0] = left
    for i in range(6):
        state_out[i : i + 1, :] = state[i]


def plan(log, state):
    return pl.pallas_call(
        plan_kernel,
        out_shape=[
            jax.ShapeDtypeStruct(log.shape, jnp.int32),
            jax.ShapeDtypeStruct(state.shape, jnp.int32),
            jax.ShapeDtypeStruct((1,), jnp.int32),
        ],
        in_specs=[SMEM, VMEM],
        out_specs=[SMEM, VMEM, SMEM],
        cost_estimate=LITTLE,
    )(log, state)


def stage_kernel(turn, count, source_ref, log_ref, cache_ref, *refs):
    arrivals = each_parcel(refs[:count])
    sends = refs[count : count + 3]
    many, _ = ROUNDS[turn]
    sent = [log_ref[SENT + PLACE[turn] + i] for i in range(3 * many)]
    begin, end = lay_out(sent, source_ref, log_ref, cache_ref, arrivals, sends, *refs[count + 3 :])
    begin()
    end()


def stage(source, log, cache, arrivals, turn):
    many, _ = ROUNDS[turn]
    return pl.pallas_call(
        functools.partial(stage_kernel, turn, len(arrivals)),
        out_shape=sends_of(many, cache),
        in_specs=[SMEM, SMEM, HBM] + [ANY] * len(arrivals),
        out_specs=[HBM] * 3,
        scratch_shapes=lay_out_scratch(many, cache),
        compiler_params=pltpu.CompilerParams(vmem_limit_bytes=VMEM_GRANT),
        cost_estimate=LITTLE,
    )(source, log, cache, *arrivals)


def late_kernel(count, source_ref, log_ref, state_ref, cache_ref, *refs):
    arrivals = each_parcel(refs[:count])
    held_in, log_out, state_out, left_out, up, down, across, held_out, store_sem, send_sem = refs[count:]
    sends = (up, down, across)
    latest = arrivals[-3:]
    place = PLACE[LAST]
    number = [log_ref[place + i] for i in range(3)]
    for i, ref in enumerate(latest):

        @pl.when(number[i] > 0)
        def _(i=i, ref=ref):
            pltpu.make_async_copy(ref, held_out.at[number[i] - 1], store_sem.at[i]).start()

    sent = [log_ref[NEXT + i] for i in range(3)]
    for i in range(3):
        parcel_from(
            sent[i], source_ref, log_ref, cache_ref, arrivals, held_in, sends[i].at[0], send_sem.at[i]
        )
    state, next_sent, next_got, left = choose([state_ref[i : i + 1, :] for i in range(6)], 1, 1, True)
    for i in range(place):
        log_out[i] = log_ref[i]
    for i in range(3):
        log_out[place + i] = log_ref[NEXT + 3 + i]
        log_out[NEXT + i] = next_sent[i]
        log_out[NEXT + 3 + i] = next_got[i]
    left_out[0] = left
    for i in range(6):
        state_out[i : i + 1, :] = state[i]
    for i in range(3):

        @pl.when(sent[i] > 0)
        def _(i=i):
            pltpu.make_async_copy(cache_ref.at[0, 0], sends[i].at[0], send_sem.at[i]).wait()

    for i, ref in enumerate(latest):

        @pl.when(number[i] > 0)
        def _(i=i, ref=ref):
            pltpu.make_async_copy(ref, held_out.at[number[i] - 1], store_sem.at[i]).wait()


def late_stage(source, log, state, cache, arrivals, held):
    count = len(arrivals)
    out = pl.pallas_call(
        functools.partial(late_kernel, count),
        out_shape=[
            jax.ShapeDtypeStruct((LOG,), jnp.int32),
            jax.ShapeDtypeStruct((8, 128), jnp.int32),
            jax.ShapeDtypeStruct((1,), jnp.int32),
        ]
        + sends_of(1, cache)
        + [jax.ShapeDtypeStruct(held.shape, held.dtype)],
        in_specs=[SMEM, SMEM, VMEM, HBM] + [ANY] * (count - 3) + [VMEM] * 3 + [HBM],
        out_specs=[SMEM, VMEM, SMEM, VMEM, VMEM, VMEM, HBM],
        scratch_shapes=[pltpu.SemaphoreType.DMA((3,)), pltpu.SemaphoreType.DMA((3,))],
        input_output_aliases={4 + count: 6},
        cost_estimate=LITTLE,
    )(source, log, state, cache, *arrivals, held)
    log, state, left, *rest = out
    return log, state, left, rest[:3], rest[3]


def room_kernel(out_ref):
    pass


def room(parcels, cache):
    return pl.pallas_call(
        room_kernel,
        out_shape=jax.ShapeDtypeStruct((parcels,) + cache.shape[2:], cache.dtype),
        out_specs=HBM,
        cost_estimate=LITTLE,
    )()


def exchange(sends):
    up, down, across = sends
    return (
        lax.ppermute(up, "cand", UP),
        lax.ppermute(down, "cand", DOWN),
        lax.ppermute(across, "cand", ACROSS),
    )


def slot_attention(q_rows, keys, values, length, score_scale):
    scores = lax.dot_general(q_rows, keys, (((1,), (1,)), ((), ())), preferred_element_type=jnp.float32)
    scores = scores * score_scale
    position = lax.broadcasted_iota(jnp.int32, scores.shape, 1)
    scores = jnp.where(position <= length, scores, -1e30)
    weights = jnp.exp(scores - jnp.max(scores, axis=1, keepdims=True))
    total = jnp.sum(weights, axis=1, keepdims=True)
    mixed = jnp.dot(weights.astype(jnp.bfloat16), values, preferred_element_type=jnp.float32)
    return mixed / total


def finish_kernel(count, *refs):
    source_ref, length_ref, log_ref, query_ref, new_ref, cache_ref = refs[:6]
    arrivals = each_parcel(refs[6 : 6 + count])
    held_ref, compacted_ref, attn_ref, rows, attn, sem, out_sem = refs[6 + count :]
    me = lax.axis_index("cand")
    slots, _, depth, width = rows.shape
    kv_heads = width // ATTN_DIM
    group = query_ref.shape[1] // width
    for s in range(slots):
        for half in range(2):
            number = (me * slots + s) * 2 + half + 1
            parcel_from(
                number, source_ref, log_ref, cache_ref, arrivals, held_ref, rows.at[s, half], sem.at[2 * s + half]
            )
    query = query_ref[...].astype(jnp.float32)
    for s in range(slots):
        length = length_ref[source_ref[me * slots + s]]
        base = pl.multiple_of((length >> 4) << 4, 16)
        for half in range(2):
            pltpu.make_async_copy(cache_ref.at[0, 0], rows.at[s, half], sem.at[2 * s + half]).wait()
            window = rows[s, half, pl.ds(base, 16), :]
            row = lax.broadcasted_iota(jnp.int32, window.shape, 0)
            fresh_row = new_ref[s, half : half + 1, :]
            rows[s, half, pl.ds(base, 16), :] = jnp.where(
                row == length - base, fresh_row.astype(jnp.float32), window.astype(jnp.float32)
            ).astype(window.dtype)
            pltpu.make_async_copy(rows.at[s, half], compacted_ref.at[s, half], out_sem.at[2 * s + half]).start()
        for k in range(kv_heads):
            columns = slice(k * ATTN_DIM, (k + 1) * ATTN_DIM)
            heads = [slice((k * group + g) * ATTN_DIM, (k * group + g + 1) * ATTN_DIM) for g in range(group)]
            mixed = slot_attention(
                jnp.concatenate([query[s : s + 1, h] for h in heads], axis=0).astype(query_ref.dtype),
                rows[s, 0, :, columns],
                rows[s, 1, :, columns],
                length,
                ATTN_DIM ** (-0.5),
            )
            for g, h in enumerate(heads):
                attn[s : s + 1, h] = mixed[g : g + 1, :]
    attn_ref[...] = attn[...].astype(attn_ref.dtype)
    for s in range(slots):
        for half in range(2):
            pltpu.make_async_copy(rows.at[s, half], compacted_ref.at[s, half], out_sem.at[2 * s + half]).wait()


def finish(source, policy_length, log, query, new, cache, arrivals, held):
    slots = query.shape[0]
    _, _, depth, width = cache.shape
    return pl.pallas_call(
        functools.partial(finish_kernel, len(arrivals)),
        out_shape=[
            jax.ShapeDtypeStruct((slots, 2, depth, width), cache.dtype),
            jax.ShapeDtypeStruct(query.shape, query.dtype),
        ],
        in_specs=[SMEM, SMEM, SMEM, VMEM, VMEM, HBM] + [ANY] * len(arrivals) + [HBM],
        out_specs=[HBM, VMEM],
        scratch_shapes=[
            pltpu.VMEM((slots, 2, depth, width), cache.dtype),
            pltpu.VMEM(query.shape, jnp.float32),
            pltpu.SemaphoreType.DMA((2 * slots,)),
            pltpu.SemaphoreType.DMA((2 * slots,)),
        ],
        compiler_params=pltpu.CompilerParams(vmem_limit_bytes=VMEM_GRANT),
        cost_estimate=LITTLE,
    )(source, policy_length, log, query, new, cache, *arrivals, held)


def routed_policy(policy_cache, policy_length, source, policy_query, policy_new, reward_inputs):
    first_log, first_state, sends = first_stage(source, policy_cache)
    arrivals = list(exchange(sends))
    log, state, left = plan(first_log, first_state)
    log, *reward_inputs = lax.optimization_barrier((log, *reward_inputs))
    give, keep = reward_share(*reward_inputs, by_core=True)
    log, give, keep = lax.optimization_barrier((log, give, keep))
    for turn in range(1, len(ROUNDS)):
        at_hand = arrivals[: 3 * sum(sent + lag <= turn for sent, (_, lag) in enumerate(ROUNDS[:turn]))]
        sends = stage(source, log, policy_cache, at_hand, turn)
        log, *sends = lax.optimization_barrier((log, *sends))
        arrivals += exchange(sends)
        if turn == 1:
            log, give = lax.optimization_barrier((log, give))
            give = lax.ppermute(give, "tp", [(0, 1), (1, 0), (2, 3), (3, 2)])
        if turn == 3:
            log, keep, give = lax.optimization_barrier((log, keep, give))
            mine, other = add_cores(keep, give)
            log, mine, other = lax.optimization_barrier((log, mine, other))
            other = lax.ppermute(other, "tp", [(0, 2), (2, 0), (1, 3), (3, 1)])
    early, latest = arrivals[:-3], arrivals[-3:]
    reward_out = (mine + other.astype(jnp.float32)).astype(jnp.bfloat16)
    left, reward_out = lax.optimization_barrier((left, reward_out))

    def unfinished(carry):
        return carry[0][0] > 0

    def one_round(carry):
        _, log, state, latest, held = carry
        log, state, left, sends, held = late_stage(source, log, state, policy_cache, early + latest, held)
        return left, log, state, list(exchange(sends)), held

    held = room(2 * SLOTS, policy_cache)
    _, log, _, latest, held = lax.while_loop(unfinished, one_round, (left, log, state, latest, held))
    compacted, attn = finish(
        source, policy_length, log, policy_query, policy_new, policy_cache, early + latest, held
    )
    return reward_out, compacted, attn


def spread_policy(policy_cache, policy_length, source, policy_query, policy_new, reward_inputs):
    reward_out = add_shares(reward_share(*reward_inputs)[0])
    attention_clusters = ASKING_UNITS // SHARED_KV_UNITS
    score_scale = ATTN_DIM ** (-0.5)
    kv_heads = policy_cache.shape[-1] // ATTN_DIM
    cache_rows = lax.iota(jnp.int32, CACHE_LENGTH)
    slot_count = policy_query.shape[0]
    per_index = policy_cache.shape[0]
    owner = source // per_index
    slots = lax.iota(jnp.int32, source.shape[0])
    earlier = (owner[:, None] == owner[None, :]) & (slots[None, :] < slots[:, None])
    rank = jnp.sum(earlier.astype(jnp.int32), axis=1)
    me = lax.axis_index("cand")
    lane = lax.iota(jnp.int32, slot_count)
    mine = (owner[None, :] == me) & (rank[None, :] == lane[:, None])
    named = jnp.sum(jnp.where(mine, source[None, :] - me * per_index, 0), axis=1)
    picked = jnp.take(policy_cache, named, axis=0)
    spread = lax.all_to_all(picked, "cand", split_axis=2, concat_axis=0, tiled=True)
    selected = jnp.take(spread, owner * slot_count + rank, axis=0)
    moved = lax.all_to_all(selected, "cand", split_axis=0, concat_axis=2, tiled=True)
    local_source = lax.dynamic_slice_in_dim(source, lax.axis_index("cand") * slot_count, slot_count)
    slot_lengths = jnp.take(policy_length, local_source)
    compacted = jnp.where(
        cache_rows[None, None, :, None] == slot_lengths[:, None, None, None],
        policy_new[:, :, None, :],
        moved,
    )
    slot_heads = policy_query.reshape(slot_count, kv_heads, attention_clusters, ATTN_DIM)
    slot_keys = compacted[:, 0].reshape(slot_count, CACHE_LENGTH, kv_heads, ATTN_DIM)
    slot_values = compacted[:, 1].reshape(slot_count, CACHE_LENGTH, kv_heads, ATTN_DIM)
    slot_scores = (
        jnp.einsum("skgd,spkd->skgp", slot_heads, slot_keys, preferred_element_type=jnp.float32)
        * score_scale
    )
    slot_visible = cache_rows[None, :] <= slot_lengths[:, None]
    slot_scores = jnp.where(slot_visible[:, None, None, :], slot_scores, -1e30)
    slot_weights = jax.nn.softmax(slot_scores, axis=-1).astype(jnp.bfloat16)
    policy_attn = jnp.einsum(
        "skgp,spkd->skgd", slot_weights, slot_values, preferred_element_type=jnp.float32
    )
    policy_attn = policy_attn.reshape(slot_count, kv_heads * attention_clusters * ATTN_DIM).astype(
        jnp.bfloat16
    )
    return reward_out, compacted, policy_attn


def reward_kernel(length_ref, query_ref, new_ref, cache_ref, weight_ref, *refs):
    out_refs = refs[:-9]
    query, new, cache, weight, rows, out, sem, weight_sem, out_sem = refs[-9:]
    candidates, tokens, units = query.shape
    depth, width = cache.shape[2:]
    kv_heads = width // ATTN_DIM
    group = units // width
    blocks, _, block = weight.shape
    scale = ATTN_DIM ** (-0.5) * LOG2_E
    token = lax.rem(lax.broadcasted_iota(jnp.int32, (group * tokens, tokens), 0), tokens)
    new_visible = lax.broadcasted_iota(jnp.int32, (group * tokens, tokens), 1) <= token
    by_rows = (((1,), (1,)), ((), ()))

    def inputs(i):
        return [
            pltpu.make_async_copy(query_ref.at[i], query.at[i], sem.at[4 * i]),
            pltpu.make_async_copy(cache_ref.at[i, 0], cache.at[i, 0], sem.at[4 * i + 1]),
            pltpu.make_async_copy(new_ref.at[i], new.at[i], sem.at[4 * i + 2]),
            pltpu.make_async_copy(cache_ref.at[i, 1], cache.at[i, 1], sem.at[4 * i + 3]),
        ]

    def fetch(j):
        first = j * block
        if len(out_refs) == 2:
            part, piece = divmod(j, blocks // 4)
            core = lax.rem(lax.axis_index("tp"), 2)
            core = 1 - core if part < 2 else core
            first = pl.multiple_of((core + 2 * (part % 2)) * (weight_ref.shape[1] // 4) + piece * block, block)
        return pltpu.make_async_copy(weight_ref.at[:, pl.ds(first, block)], weight.at[j], weight_sem.at[j])

    def put(j):
        target = out_refs[0].at[:, pl.ds(j * block, block)] if len(out_refs) == 1 else None
        if target is None:
            part, piece = divmod(j, blocks // 4)
            target = out_refs[part // 2].at[part % 2, :, pl.ds(piece * block, block)]
        return pltpu.make_async_copy(out.at[j % 2], target, out_sem.at[j % 2])

    for i in range(min(3, candidates)):
        for copy in inputs(i):
            copy.start()
    fetched = 0
    for i in range(candidates):
        for copy in inputs(i):
            copy.wait()
        if i + 3 < candidates:
            for copy in inputs(i + 3):
                copy.start()
        while fetched < blocks * (i + 1) // candidates:
            fetch(fetched).start()
            fetched += 1
        visible = lax.broadcasted_iota(jnp.int32, (1, depth), 1) < length_ref[i]
        for k in range(kv_heads):
            columns = slice(k * ATTN_DIM, (k + 1) * ATTN_DIM)
            heads = [slice((k * group + g) * ATTN_DIM, (k * group + g + 1) * ATTN_DIM) for g in range(group)]
            asked = jnp.concatenate([query[i, :, h] for h in heads], axis=0)
            old = lax.dot_general(asked, cache[i, 0, :, columns], by_rows, preferred_element_type=jnp.float32)
            fresh = lax.dot_general(asked, new[i, 0, :, columns], by_rows, preferred_element_type=jnp.float32)
            old = jnp.where(visible, old, -1e30)
            fresh = jnp.where(new_visible, fresh, -1e30)
            peak = jnp.maximum(jnp.max(old, axis=1, keepdims=True), jnp.max(fresh, axis=1, keepdims=True))
            old = jnp.exp2((old - peak) * scale)
            fresh = jnp.exp2((fresh - peak) * scale)
            total = jnp.sum(old, axis=1, keepdims=True) + jnp.sum(fresh, axis=1, keepdims=True)
            mixed = jnp.dot(old.astype(jnp.bfloat16), cache[i, 1, :, columns], preferred_element_type=jnp.float32)
            mixed += jnp.dot(fresh.astype(jnp.bfloat16), new[i, 1, :, columns], preferred_element_type=jnp.float32)
            mixed = (mixed / total).astype(rows.dtype)
            for g, h in enumerate(heads):
                rows[i * tokens : (i + 1) * tokens, h] = mixed[g * tokens : (g + 1) * tokens, :]
    for j in range(blocks):
        fetch(j).wait()
        if j >= 2:
            put(j - 2).wait()
        out[j % 2] = jnp.dot(rows[...], weight[j], preferred_element_type=jnp.float32)
        put(j).start()
    put(blocks - 2).wait()
    put(blocks - 1).wait()


def reward_share(query, new, cache, length, weight, by_core=False):
    candidates, tokens, units = query.shape
    features = weight.shape[1]
    block = 512
    shape = (2, candidates * tokens, features // 4) if by_core else (candidates * tokens, features)
    outputs = 2 if by_core else 1
    return pl.pallas_call(
        reward_kernel,
        out_shape=[jax.ShapeDtypeStruct(shape, jnp.float32)] * outputs,
        in_specs=[SMEM, HBM, HBM, HBM, HBM],
        out_specs=[HBM] * outputs,
        scratch_shapes=[
            pltpu.VMEM(query.shape, query.dtype),
            pltpu.VMEM(new.shape, new.dtype),
            pltpu.VMEM(cache.shape, cache.dtype),
            pltpu.VMEM((features // block, units, block), weight.dtype),
            pltpu.VMEM((candidates * tokens, units), query.dtype),
            pltpu.VMEM((2, candidates * tokens, block), jnp.float32),
            pltpu.SemaphoreType.DMA((4 * candidates,)),
            pltpu.SemaphoreType.DMA((features // block,)),
            pltpu.SemaphoreType.DMA((2,)),
        ],
        compiler_params=pltpu.CompilerParams(vmem_limit_bytes=VMEM_GRANT),
        cost_estimate=LITTLE,
    )(length, query, new, cache, weight)


def add_cores_kernel(keep_ref, got_ref, mine_ref, other_ref, keep, got, out, sem, out_sem):
    x = lax.axis_index("tp") // 2
    for i, part in enumerate((1 - x, x)):
        pltpu.make_async_copy(keep_ref.at[part], keep.at[i], sem.at[2 * i]).start()
        pltpu.make_async_copy(got_ref.at[part], got.at[i], sem.at[2 * i + 1]).start()
    for i, part in enumerate((1 - x, x)):
        pltpu.make_async_copy(keep_ref.at[part], keep.at[i], sem.at[2 * i]).wait()
        pltpu.make_async_copy(got_ref.at[part], got.at[i], sem.at[2 * i + 1]).wait()
        if i == 0:
            out[...] = (keep[i] + got[i]).astype(out.dtype)
            pltpu.make_async_copy(out, other_ref, out_sem.at[0]).start()
        else:
            keep[i] += got[i]
            pltpu.make_async_copy(keep.at[i], mine_ref, out_sem.at[1]).start()
    pltpu.make_async_copy(out, other_ref, out_sem.at[0]).wait()
    pltpu.make_async_copy(keep.at[1], mine_ref, out_sem.at[1]).wait()


def add_cores(keep, got):
    part = keep.shape[1:]
    return pl.pallas_call(
        add_cores_kernel,
        out_shape=[jax.ShapeDtypeStruct(part, jnp.float32), jax.ShapeDtypeStruct(part, jnp.bfloat16)],
        in_specs=[HBM, HBM],
        out_specs=[HBM, HBM],
        scratch_shapes=[
            pltpu.VMEM(keep.shape, jnp.float32),
            pltpu.VMEM(keep.shape, jnp.float32),
            pltpu.VMEM(part, jnp.bfloat16),
            pltpu.SemaphoreType.DMA((4,)),
            pltpu.SemaphoreType.DMA((2,)),
        ],
        compiler_params=pltpu.CompilerParams(vmem_limit_bytes=VMEM_GRANT),
        cost_estimate=LITTLE,
    )(keep, got)


def add_shares(share):
    return lax.psum_scatter(share, "tp", scatter_dimension=1, tiled=True).astype(jnp.bfloat16)


def body(
    cand_count,
    tp_count,
    reward_query,
    reward_new,
    reward_key_value_cache,
    reward_length,
    out_weight,
    policy_cache,
    policy_length,
    source,
    policy_query,
    policy_new,
):
    policy = spread_policy
    if (cand_count, tp_count, policy_cache.shape[0], source.shape[0]) == (GRID, 4, 8, SLOTS):
        policy = routed_policy
    reward_inputs = (reward_query, reward_new, reward_key_value_cache, reward_length, out_weight)
    return policy(policy_cache, policy_length, source, policy_query, policy_new, reward_inputs)


def solution(mesh):
    in_specs = (
        P("cand", None, "tp"),
        P("cand", None, None, "tp"),
        P("cand", None, None, "tp"),
        P("cand"),
        P("tp", None),
        P("cand", None, None, "tp"),
        P(),
        P(),
        P("cand", "tp"),
        P("cand", None, "tp"),
    )
    out_specs = (P("cand", "tp"), P("cand", None, None, "tp"), P("cand", "tp"))
    return jax.shard_map(
        functools.partial(body, mesh.shape["cand"], mesh.shape["tp"]),
        mesh=mesh,
        in_specs=in_specs,
        out_specs=out_specs,
        check_vma=False,
    )
```

```python
import functools

import jax
import jax.numpy as jnp
from jax import lax
from jax.experimental import pallas as pl
from jax.experimental.pallas import tpu as pltpu
from jax.sharding import PartitionSpec as P

ASKING_UNITS = 64
SHARED_KV_UNITS = 8
ATTN_DIM = 128
NEW_TOKEN_COUNT = 32
CACHE_LENGTH = 768

GRID_Z = 4
GRID_Y = 2
GRID = GRID_Z * GRID_Y
ROUNDS = [(2, 1, True)] + [(1, 2, turn not in (3, 4)) for turn in range(1, 9)]
LAST = len(ROUNDS) - 1
PLACE = [3 * sum(many for many, _, _ in ROUNDS[:turn]) for turn in range(len(ROUNDS) + 1)]
SENT = PLACE[-1]
NEXT = 2 * SENT
LOG = 128
SLOTS = 4 * GRID
UP = [(n, n + 2) for n in range(6)]
DOWN = [(n + 2, n) for n in range(6)]
ACROSS = [(n, n + 1 - 2 * (n % 2)) for n in range(8)]

VMEM_GRANT = 60 * 1024 * 1024
LOG2_E = 1.4426950408889634

ANY = pl.BlockSpec(memory_space=pl.ANY)
HBM = pl.BlockSpec(memory_space=pltpu.HBM)
SMEM = pl.BlockSpec(memory_space=pltpu.SMEM)
VMEM = pl.BlockSpec(memory_space=pltpu.VMEM)
LITTLE = pl.CostEstimate(flops=1000, bytes_accessed=1000, transcendentals=0)


def choose(state, many, lag, use_across=True, open_all=False):
    z, y, wait, last_z, last_y, lane_y = state
    me = lax.axis_index("cand")
    need_z = z != last_z
    next_y = jnp.where(need_z, lane_y, last_y)
    move_y = y != next_y
    move = jnp.where(move_y, 2, jnp.where(need_z, jnp.where(last_z > z, 0, 1), 3))
    after = jnp.where(need_z & (lane_y != last_y), 1, 0)
    steps = jnp.abs(z - last_z) + jnp.where(move_y, 1, 0) + after
    left = jnp.sum(jnp.where(move < 3, 1.0, 0.0)).astype(jnp.int32)
    ready = move < 3
    if not open_all:
        ready = ready & (wait <= 0)
    if not use_across:
        ready = ready & (move != 2)
    link = jnp.where(ready, move * GRID + z * GRID_Y + y, 99)
    column = lax.broadcasted_iota(jnp.int32, (1, 128), 1)
    key = (steps * 128 + 127 - column).astype(jnp.float32)
    rows = lax.broadcasted_iota(jnp.int32, (3 * GRID, 128), 0)
    names = (lax.broadcasted_iota(jnp.int32, (3 * GRID, 128), 1) + 1).astype(jnp.float32)
    keys = jnp.where(rows == link, key, -1.0)
    partner = me + 1 - 2 * lax.rem(me, 2)
    out_scale = (
        jnp.where(rows == me, 1.0, 0.0)
        + jnp.where(rows == me + GRID, 128.0, 0.0)
        + jnp.where(rows == me + 2 * GRID, 16384.0, 0.0)
    )
    in_scale = (
        jnp.where(rows == me - 2, 1.0, 0.0)
        + jnp.where((rows == me + 2 + GRID) & (rows < 2 * GRID), 128.0, 0.0)
        + jnp.where(rows == partner + 2 * GRID, 16384.0, 0.0)
    )
    moved = jnp.zeros_like(key)
    sent, got = [], []
    for _ in range(many):
        best = jnp.max(keys, axis=1, keepdims=True)
        won = (keys == best) & (keys >= 0.0)
        number = jnp.where(won, names, 0.0)
        keys = jnp.where(won, -1.0, keys)
        moved = jnp.maximum(moved, jnp.max(number, axis=0, keepdims=True))
        for packed, into in ((jnp.sum(number * out_scale), sent), (jnp.sum(number * in_scale), got)):
            packed = packed.astype(jnp.int32)
            into += [packed & 127, (packed >> 7) & 127, packed >> 14]
    moved = moved > 0.0
    z = jnp.where(moved, z + jnp.where(move == 0, 1, 0) - jnp.where(move == 1, 1, 0), z)
    y = jnp.where(moved & (move == 2), 1 - y, y)
    wait = jnp.where(moved, lag - 1, jnp.maximum(wait - 1, 0))
    return [z, y, wait, last_z, last_y, lane_y], sent, got, left


def parcel_from(number, source_ref, log_ref, cache_ref, arrivals, held_ref, target, sem):
    index = number - 1
    slot, half = index >> 1, index & 1
    per_index = cache_ref.shape[0]
    local = source_ref[jnp.maximum(slot, 0)] - lax.axis_index("cand") * per_index
    own = (number > 0) & (local >= 0) & (local < per_index)
    elsewhere = (number > 0) & jnp.logical_not(own)

    @pl.when(own)
    def _():
        pltpu.make_async_copy(cache_ref.at[local, half], target, sem).start()

    for i, ref in enumerate(arrivals):
        match = elsewhere & (log_ref[i] == number)
        if held_ref is not None:
            elsewhere = elsewhere & (log_ref[i] != number)

        @pl.when(match)
        def _(ref=ref):
            pltpu.make_async_copy(ref, target, sem).start()

    if held_ref is not None:

        @pl.when(elsewhere)
        def _():
            pltpu.make_async_copy(held_ref.at[index], target, sem).start()


def each_parcel(arrivals):
    parcels = []
    for first in range(0, len(arrivals), 3):
        triple = arrivals[first : first + 3]
        parcels += [ref.at[i] for i in range(triple[0].shape[0]) for ref in triple]
    return parcels


def lay_out(numbers, source_ref, log_ref, cache_ref, arrivals, sends, room, in_sem, out_sem):
    many = sends[0].shape[0]

    def put(i):
        return pltpu.make_async_copy(room.at[i], sends[i % 3].at[i // 3], out_sem.at[i])

    def begin():
        for i in range(3 * many):
            parcel_from(numbers[i], source_ref, log_ref, cache_ref, arrivals, None, room.at[i], in_sem.at[i])

    def end():
        for i in range(3 * many):

            @pl.when(numbers[i] > 0)
            def _(i=i):
                pltpu.make_async_copy(cache_ref.at[0, 0], room.at[i], in_sem.at[i]).wait()
                put(i).start()

        for i in range(3 * many):

            @pl.when(numbers[i] > 0)
            def _(i=i):
                put(i).wait()

    return begin, end


def lay_out_scratch(many, cache):
    return [
        pltpu.VMEM((3 * many,) + cache.shape[2:], cache.dtype),
        pltpu.SemaphoreType.DMA((3 * many,)),
        pltpu.SemaphoreType.DMA((3 * many,)),
    ]


def sends_of(many, cache):
    return [jax.ShapeDtypeStruct((many,) + cache.shape[2:], cache.dtype)] * 3


def first_kernel(source_ref, cache_ref, log_out, state_out, up, down, across, *scratch):
    parcel = lax.broadcasted_iota(jnp.int32, (1, 128), 1)
    owner = jnp.zeros_like(parcel)
    for i in range(SLOTS):
        owner = jnp.where((parcel >> 1) == i, source_ref[i] >> 3, owner)
    target = jnp.where(parcel < 2 * SLOTS, parcel >> 3, 0)
    aligned = []
    crossing = {}
    for i in range(SLOTS):
        last_z, last_y = divmod(i // (SLOTS // GRID), GRID_Y)
        first = source_ref[i] >> 3
        same = (first & 1) == last_y
        across_middle = same & (((first >> 2) == 1) != (last_z >= 2))
        before = crossing.get((last_z >= 2, last_y), 0)
        crossing[last_z >= 2, last_y] = before + across_middle.astype(jnp.int32)
        aligned.append((same, across_middle, before, last_z >= 2, last_y))
    lane = parcel & 1
    for i, (same, across_middle, before, half, last_y) in enumerate(aligned):
        fewer = jnp.minimum(crossing[half, 0], crossing[half, 1])
        stays = same & jnp.logical_not(across_middle & (before >= fewer))
        lane = jnp.where((parcel >> 1) == jnp.where(stays, i, -1), last_y, lane)
    state = [owner >> 1, owner & 1, jnp.zeros_like(parcel), target >> 1, target & 1, lane]
    state, sent, got, _ = choose(state, *ROUNDS[0])
    begin, end = lay_out(sent, source_ref, None, cache_ref, [], (up, down, across), *scratch)
    begin()
    for i in range(LOG):
        log_out[i] = 0
    for i in range(len(got)):
        log_out[i] = got[i]
        log_out[SENT + i] = sent[i]
    for i in range(6):
        state_out[i : i + 1, :] = state[i]
    end()


def first_stage(source, cache):
    many, _, _ = ROUNDS[0]
    log, state, *sends = pl.pallas_call(
        first_kernel,
        out_shape=[jax.ShapeDtypeStruct((LOG,), jnp.int32), jax.ShapeDtypeStruct((8, 128), jnp.int32)]
        + sends_of(many, cache),
        in_specs=[SMEM, HBM],
        out_specs=[SMEM, VMEM, HBM, HBM, HBM],
        scratch_shapes=lay_out_scratch(many, cache),
        compiler_params=pltpu.CompilerParams(vmem_limit_bytes=VMEM_GRANT),
        cost_estimate=LITTLE,
    )(source, cache)
    return log, state, sends


def plan_kernel(log_ref, state_ref, log_out, state_out, left_out):
    state = [state_ref[i : i + 1, :] for i in range(6)]
    for i in range(LOG):
        log_out[i] = log_ref[i]
    for turn in range(1, len(ROUNDS)):
        state, sent, got, _ = choose(state, *ROUNDS[turn])
        for i in range(len(got)):
            log_out[PLACE[turn] + i] = got[i]
            log_out[SENT + PLACE[turn] + i] = sent[i]
    state, sent, got, left = choose(state, 1, 1, open_all=True)
    for i in range(3):
        log_out[NEXT + i] = sent[i]
        log_out[NEXT + 3 + i] = got[i]
    left_out[0] = left
    for i in range(6):
        state_out[i : i + 1, :] = state[i]


def plan(log, state):
    return pl.pallas_call(
        plan_kernel,
        out_shape=[
            jax.ShapeDtypeStruct(log.shape, jnp.int32),
            jax.ShapeDtypeStruct(state.shape, jnp.int32),
            jax.ShapeDtypeStruct((1,), jnp.int32),
        ],
        in_specs=[SMEM, VMEM],
        out_specs=[SMEM, VMEM, SMEM],
        cost_estimate=LITTLE,
    )(log, state)


def stage_kernel(turn, count, source_ref, log_ref, cache_ref, *refs):
    arrivals = each_parcel(refs[:count])
    sends = refs[count : count + 3]
    many, _, _ = ROUNDS[turn]
    sent = [log_ref[SENT + PLACE[turn] + i] for i in range(3 * many)]
    begin, end = lay_out(sent, source_ref, log_ref, cache_ref, arrivals, sends, *refs[count + 3 :])
    begin()
    end()


def stage(source, log, cache, arrivals, turn):
    many, _, _ = ROUNDS[turn]
    return pl.pallas_call(
        functools.partial(stage_kernel, turn, len(arrivals)),
        out_shape=sends_of(many, cache),
        in_specs=[SMEM, SMEM, HBM] + [ANY] * len(arrivals),
        out_specs=[HBM] * 3,
        scratch_shapes=lay_out_scratch(many, cache),
        compiler_params=pltpu.CompilerParams(vmem_limit_bytes=VMEM_GRANT),
        cost_estimate=LITTLE,
    )(source, log, cache, *arrivals)


def late_kernel(count, source_ref, log_ref, state_ref, cache_ref, *refs):
    arrivals = each_parcel(refs[:count])
    held_in, log_out, state_out, left_out, up, down, across, held_out, store_sem, send_sem = refs[count:]
    sends = (up, down, across)
    latest = arrivals[-3:]
    place = PLACE[LAST]
    number = [log_ref[place + i] for i in range(3)]
    for i, ref in enumerate(latest):

        @pl.when(number[i] > 0)
        def _(i=i, ref=ref):
            pltpu.make_async_copy(ref, held_out.at[number[i] - 1], store_sem.at[i]).start()

    sent = [log_ref[NEXT + i] for i in range(3)]
    for i in range(3):
        parcel_from(
            sent[i], source_ref, log_ref, cache_ref, arrivals, held_in, sends[i].at[0], send_sem.at[i]
        )
    state, next_sent, next_got, left = choose(
        [state_ref[i : i + 1, :] for i in range(6)], 1, 1, open_all=True
    )
    for i in range(place):
        log_out[i] = log_ref[i]
    for i in range(3):
        log_out[place + i] = log_ref[NEXT + 3 + i]
        log_out[NEXT + i] = next_sent[i]
        log_out[NEXT + 3 + i] = next_got[i]
    left_out[0] = left
    for i in range(6):
        state_out[i : i + 1, :] = state[i]
    for i in range(3):

        @pl.when(sent[i] > 0)
        def _(i=i):
            pltpu.make_async_copy(cache_ref.at[0, 0], sends[i].at[0], send_sem.at[i]).wait()

    for i, ref in enumerate(latest):

        @pl.when(number[i] > 0)
        def _(i=i, ref=ref):
            pltpu.make_async_copy(ref, held_out.at[number[i] - 1], store_sem.at[i]).wait()


def late_stage(source, log, state, cache, arrivals, held):
    count = len(arrivals)
    out = pl.pallas_call(
        functools.partial(late_kernel, count),
        out_shape=[
            jax.ShapeDtypeStruct((LOG,), jnp.int32),
            jax.ShapeDtypeStruct((8, 128), jnp.int32),
            jax.ShapeDtypeStruct((1,), jnp.int32),
        ]
        + sends_of(1, cache)
        + [jax.ShapeDtypeStruct(held.shape, held.dtype)],
        in_specs=[SMEM, SMEM, VMEM, HBM] + [ANY] * (count - 3) + [VMEM] * 3 + [HBM],
        out_specs=[SMEM, VMEM, SMEM, VMEM, VMEM, VMEM, HBM],
        scratch_shapes=[pltpu.SemaphoreType.DMA((3,)), pltpu.SemaphoreType.DMA((3,))],
        input_output_aliases={4 + count: 6},
        cost_estimate=LITTLE,
    )(source, log, state, cache, *arrivals, held)
    log, state, left, *rest = out
    return log, state, left, rest[:3], rest[3]


def room_kernel(out_ref):
    pass


def room(parcels, cache):
    return pl.pallas_call(
        room_kernel,
        out_shape=jax.ShapeDtypeStruct((parcels,) + cache.shape[2:], cache.dtype),
        out_specs=HBM,
        cost_estimate=LITTLE,
    )()


def exchange(sends, use_across=True):
    up, down, across = sends
    up = lax.ppermute(up, "cand", UP)
    down = lax.ppermute(down, "cand", DOWN)
    return up, down, lax.ppermute(across, "cand", ACROSS) if use_across else down


def slot_attention(q_rows, keys, values, length, score_scale):
    scores = lax.dot_general(q_rows, keys, (((1,), (1,)), ((), ())), preferred_element_type=jnp.float32)
    scores = scores * score_scale
    position = lax.broadcasted_iota(jnp.int32, scores.shape, 1)
    scores = jnp.where(position <= length, scores, -1e30)
    weights = jnp.exp(scores - jnp.max(scores, axis=1, keepdims=True))
    total = jnp.sum(weights, axis=1, keepdims=True)
    mixed = jnp.dot(weights.astype(jnp.bfloat16), values, preferred_element_type=jnp.float32)
    return mixed / total


def finish_kernel(count, *refs):
    source_ref, length_ref, log_ref, query_ref, new_ref, cache_ref = refs[:6]
    arrivals = each_parcel(refs[6 : 6 + count])
    held_ref, compacted_ref, attn_ref, rows, attn, sem, out_sem = refs[6 + count :]
    me = lax.axis_index("cand")
    slots, _, depth, width = rows.shape
    kv_heads = width // ATTN_DIM
    group = query_ref.shape[1] // width
    for s in range(slots):
        for half in range(2):
            number = (me * slots + s) * 2 + half + 1
            parcel_from(
                number, source_ref, log_ref, cache_ref, arrivals, held_ref, rows.at[s, half], sem.at[2 * s + half]
            )
    query = query_ref[...].astype(jnp.float32)
    for s in range(slots):
        length = length_ref[source_ref[me * slots + s]]
        base = pl.multiple_of((length >> 4) << 4, 16)
        for half in range(2):
            pltpu.make_async_copy(cache_ref.at[0, 0], rows.at[s, half], sem.at[2 * s + half]).wait()
            window = rows[s, half, pl.ds(base, 16), :]
            row = lax.broadcasted_iota(jnp.int32, window.shape, 0)
            fresh_row = new_ref[s, half : half + 1, :]
            rows[s, half, pl.ds(base, 16), :] = jnp.where(
                row == length - base, fresh_row.astype(jnp.float32), window.astype(jnp.float32)
            ).astype(window.dtype)
            pltpu.make_async_copy(rows.at[s, half], compacted_ref.at[s, half], out_sem.at[2 * s + half]).start()
        for k in range(kv_heads):
            columns = slice(k * ATTN_DIM, (k + 1) * ATTN_DIM)
            heads = [slice((k * group + g) * ATTN_DIM, (k * group + g + 1) * ATTN_DIM) for g in range(group)]
            mixed = slot_attention(
                jnp.concatenate([query[s : s + 1, h] for h in heads], axis=0).astype(query_ref.dtype),
                rows[s, 0, :, columns],
                rows[s, 1, :, columns],
                length,
                ATTN_DIM ** (-0.5),
            )
            for g, h in enumerate(heads):
                attn[s : s + 1, h] = mixed[g : g + 1, :]
    attn_ref[...] = attn[...].astype(attn_ref.dtype)
    for s in range(slots):
        for half in range(2):
            pltpu.make_async_copy(rows.at[s, half], compacted_ref.at[s, half], out_sem.at[2 * s + half]).wait()


def finish(source, policy_length, log, query, new, cache, arrivals, held):
    slots = query.shape[0]
    _, _, depth, width = cache.shape
    return pl.pallas_call(
        functools.partial(finish_kernel, len(arrivals)),
        out_shape=[
            jax.ShapeDtypeStruct((slots, 2, depth, width), cache.dtype),
            jax.ShapeDtypeStruct(query.shape, query.dtype),
        ],
        in_specs=[SMEM, SMEM, SMEM, VMEM, VMEM, HBM] + [ANY] * len(arrivals) + [HBM],
        out_specs=[HBM, VMEM],
        scratch_shapes=[
            pltpu.VMEM((slots, 2, depth, width), cache.dtype),
            pltpu.VMEM(query.shape, jnp.float32),
            pltpu.SemaphoreType.DMA((2 * slots,)),
            pltpu.SemaphoreType.DMA((2 * slots,)),
        ],
        compiler_params=pltpu.CompilerParams(vmem_limit_bytes=VMEM_GRANT),
        cost_estimate=LITTLE,
    )(source, policy_length, log, query, new, cache, *arrivals, held)


def routed_policy(policy_cache, policy_length, source, policy_query, policy_new, reward_inputs):
    first_log, first_state, sends = first_stage(source, policy_cache)
    arrivals = list(exchange(sends))
    log, state, left = plan(first_log, first_state)
    log, *reward_inputs = lax.optimization_barrier((log, *reward_inputs))
    give, keep = reward_share(*reward_inputs, by_core=True)
    log, give, keep = lax.optimization_barrier((log, give, keep))
    for turn in range(1, len(ROUNDS)):
        at_hand = arrivals[: 3 * sum(sent + lag <= turn for sent, (_, lag, _) in enumerate(ROUNDS[:turn]))]
        sends = stage(source, log, policy_cache, at_hand, turn)
        log, *sends = lax.optimization_barrier((log, *sends))
        arrivals += exchange(sends, ROUNDS[turn][2])
        if turn == 1:
            log, give = lax.optimization_barrier((log, give))
            give = lax.ppermute(give, "tp", [(0, 1), (1, 0), (2, 3), (3, 2)])
        if turn == 3:
            log, keep, give = lax.optimization_barrier((log, keep, give))
            mine, other = add_cores(keep, give)
            log, mine, other = lax.optimization_barrier((log, mine, other))
            other = lax.ppermute(other, "tp", [(0, 2), (2, 0), (1, 3), (3, 1)])
    early, latest = arrivals[:-3], arrivals[-3:]
    reward_out = (mine + other.astype(jnp.float32)).astype(jnp.bfloat16)
    left, reward_out = lax.optimization_barrier((left, reward_out))

    def unfinished(carry):
        return carry[0][0] > 0

    def one_round(carry):
        _, log, state, latest, held = carry
        log, state, left, sends, held = late_stage(source, log, state, policy_cache, early + latest, held)
        return left, log, state, list(exchange(sends)), held

    held = room(2 * SLOTS, policy_cache)
    _, log, _, latest, held = lax.while_loop(unfinished, one_round, (left, log, state, latest, held))
    compacted, attn = finish(
        source, policy_length, log, policy_query, policy_new, policy_cache, early + latest, held
    )
    return reward_out, compacted, attn


def spread_policy(policy_cache, policy_length, source, policy_query, policy_new, reward_inputs):
    reward_out = add_shares(reward_share(*reward_inputs)[0])
    attention_clusters = ASKING_UNITS // SHARED_KV_UNITS
    score_scale = ATTN_DIM ** (-0.5)
    kv_heads = policy_cache.shape[-1] // ATTN_DIM
    cache_rows = lax.iota(jnp.int32, CACHE_LENGTH)
    slot_count = policy_query.shape[0]
    per_index = policy_cache.shape[0]
    owner = source // per_index
    slots = lax.iota(jnp.int32, source.shape[0])
    earlier = (owner[:, None] == owner[None, :]) & (slots[None, :] < slots[:, None])
    rank = jnp.sum(earlier.astype(jnp.int32), axis=1)
    me = lax.axis_index("cand")
    lane = lax.iota(jnp.int32, slot_count)
    mine = (owner[None, :] == me) & (rank[None, :] == lane[:, None])
    named = jnp.sum(jnp.where(mine, source[None, :] - me * per_index, 0), axis=1)
    picked = jnp.take(policy_cache, named, axis=0)
    spread = lax.all_to_all(picked, "cand", split_axis=2, concat_axis=0, tiled=True)
    selected = jnp.take(spread, owner * slot_count + rank, axis=0)
    moved = lax.all_to_all(selected, "cand", split_axis=0, concat_axis=2, tiled=True)
    local_source = lax.dynamic_slice_in_dim(source, lax.axis_index("cand") * slot_count, slot_count)
    slot_lengths = jnp.take(policy_length, local_source)
    compacted = jnp.where(
        cache_rows[None, None, :, None] == slot_lengths[:, None, None, None],
        policy_new[:, :, None, :],
        moved,
    )
    slot_heads = policy_query.reshape(slot_count, kv_heads, attention_clusters, ATTN_DIM)
    slot_keys = compacted[:, 0].reshape(slot_count, CACHE_LENGTH, kv_heads, ATTN_DIM)
    slot_values = compacted[:, 1].reshape(slot_count, CACHE_LENGTH, kv_heads, ATTN_DIM)
    slot_scores = (
        jnp.einsum("skgd,spkd->skgp", slot_heads, slot_keys, preferred_element_type=jnp.float32)
        * score_scale
    )
    slot_visible = cache_rows[None, :] <= slot_lengths[:, None]
    slot_scores = jnp.where(slot_visible[:, None, None, :], slot_scores, -1e30)
    slot_weights = jax.nn.softmax(slot_scores, axis=-1).astype(jnp.bfloat16)
    policy_attn = jnp.einsum(
        "skgp,spkd->skgd", slot_weights, slot_values, preferred_element_type=jnp.float32
    )
    policy_attn = policy_attn.reshape(slot_count, kv_heads * attention_clusters * ATTN_DIM).astype(
        jnp.bfloat16
    )
    return reward_out, compacted, policy_attn


def reward_kernel(length_ref, query_ref, new_ref, cache_ref, weight_ref, *refs):
    out_refs = refs[:-9]
    query, new, cache, weight, rows, out, sem, weight_sem, out_sem = refs[-9:]
    candidates, tokens, units = query.shape
    depth, width = cache.shape[2:]
    kv_heads = width // ATTN_DIM
    group = units // width
    blocks, _, block = weight.shape
    scale = ATTN_DIM ** (-0.5) * LOG2_E
    token = lax.rem(lax.broadcasted_iota(jnp.int32, (group * tokens, tokens), 0), tokens)
    new_visible = lax.broadcasted_iota(jnp.int32, (group * tokens, tokens), 1) <= token
    by_rows = (((1,), (1,)), ((), ()))

    def inputs(i):
        return [
            pltpu.make_async_copy(query_ref.at[i], query.at[i], sem.at[4 * i]),
            pltpu.make_async_copy(cache_ref.at[i, 0], cache.at[i, 0], sem.at[4 * i + 1]),
            pltpu.make_async_copy(new_ref.at[i], new.at[i], sem.at[4 * i + 2]),
            pltpu.make_async_copy(cache_ref.at[i, 1], cache.at[i, 1], sem.at[4 * i + 3]),
        ]

    def fetch(j):
        first = j * block
        if len(out_refs) == 2:
            part, piece = divmod(j, blocks // 4)
            core = lax.rem(lax.axis_index("tp"), 2)
            core = 1 - core if part < 2 else core
            first = pl.multiple_of((core + 2 * (part % 2)) * (weight_ref.shape[1] // 4) + piece * block, block)
        return pltpu.make_async_copy(weight_ref.at[:, pl.ds(first, block)], weight.at[j], weight_sem.at[j])

    def put(j):
        target = out_refs[0].at[:, pl.ds(j * block, block)] if len(out_refs) == 1 else None
        if target is None:
            part, piece = divmod(j, blocks // 4)
            target = out_refs[part // 2].at[part % 2, :, pl.ds(piece * block, block)]
        return pltpu.make_async_copy(out.at[j % 2], target, out_sem.at[j % 2])

    for i in range(min(3, candidates)):
        for copy in inputs(i):
            copy.start()
    fetched = 0
    for i in range(candidates):
        for copy in inputs(i):
            copy.wait()
        if i + 3 < candidates:
            for copy in inputs(i + 3):
                copy.start()
        while fetched < blocks * (i + 1) // candidates:
            fetch(fetched).start()
            fetched += 1
        visible = lax.broadcasted_iota(jnp.int32, (1, depth), 1) < length_ref[i]
        for k in range(kv_heads):
            columns = slice(k * ATTN_DIM, (k + 1) * ATTN_DIM)
            heads = [slice((k * group + g) * ATTN_DIM, (k * group + g + 1) * ATTN_DIM) for g in range(group)]
            asked = jnp.concatenate([query[i, :, h] for h in heads], axis=0)
            old = lax.dot_general(asked, cache[i, 0, :, columns], by_rows, preferred_element_type=jnp.float32)
            fresh = lax.dot_general(asked, new[i, 0, :, columns], by_rows, preferred_element_type=jnp.float32)
            old = jnp.where(visible, old, -1e30)
            fresh = jnp.where(new_visible, fresh, -1e30)
            peak = jnp.maximum(jnp.max(old, axis=1, keepdims=True), jnp.max(fresh, axis=1, keepdims=True))
            old = jnp.exp2((old - peak) * scale)
            fresh = jnp.exp2((fresh - peak) * scale)
            total = jnp.sum(old, axis=1, keepdims=True) + jnp.sum(fresh, axis=1, keepdims=True)
            mixed = jnp.dot(old.astype(jnp.bfloat16), cache[i, 1, :, columns], preferred_element_type=jnp.float32)
            mixed += jnp.dot(fresh.astype(jnp.bfloat16), new[i, 1, :, columns], preferred_element_type=jnp.float32)
            mixed = (mixed / total).astype(rows.dtype)
            for g, h in enumerate(heads):
                rows[i * tokens : (i + 1) * tokens, h] = mixed[g * tokens : (g + 1) * tokens, :]
    for j in range(blocks):
        fetch(j).wait()
        if j >= 2:
            put(j - 2).wait()
        out[j % 2] = jnp.dot(rows[...], weight[j], preferred_element_type=jnp.float32)
        put(j).start()
    put(blocks - 2).wait()
    put(blocks - 1).wait()


def reward_share(query, new, cache, length, weight, by_core=False):
    candidates, tokens, units = query.shape
    features = weight.shape[1]
    block = 512
    shape = (2, candidates * tokens, features // 4) if by_core else (candidates * tokens, features)
    outputs = 2 if by_core else 1
    return pl.pallas_call(
        reward_kernel,
        out_shape=[jax.ShapeDtypeStruct(shape, jnp.float32)] * outputs,
        in_specs=[SMEM, HBM, HBM, HBM, HBM],
        out_specs=[HBM] * outputs,
        scratch_shapes=[
            pltpu.VMEM(query.shape, query.dtype),
            pltpu.VMEM(new.shape, new.dtype),
            pltpu.VMEM(cache.shape, cache.dtype),
            pltpu.VMEM((features // block, units, block), weight.dtype),
            pltpu.VMEM((candidates * tokens, units), query.dtype),
            pltpu.VMEM((2, candidates * tokens, block), jnp.float32),
            pltpu.SemaphoreType.DMA((4 * candidates,)),
            pltpu.SemaphoreType.DMA((features // block,)),
            pltpu.SemaphoreType.DMA((2,)),
        ],
        compiler_params=pltpu.CompilerParams(vmem_limit_bytes=VMEM_GRANT),
        cost_estimate=LITTLE,
    )(length, query, new, cache, weight)


def add_cores_kernel(keep_ref, got_ref, mine_ref, other_ref, keep, got, out, sem, out_sem):
    x = lax.axis_index("tp") // 2
    for i, part in enumerate((1 - x, x)):
        pltpu.make_async_copy(keep_ref.at[part], keep.at[i], sem.at[2 * i]).start()
        pltpu.make_async_copy(got_ref.at[part], got.at[i], sem.at[2 * i + 1]).start()
    for i, part in enumerate((1 - x, x)):
        pltpu.make_async_copy(keep_ref.at[part], keep.at[i], sem.at[2 * i]).wait()
        pltpu.make_async_copy(got_ref.at[part], got.at[i], sem.at[2 * i + 1]).wait()
        if i == 0:
            out[...] = (keep[i] + got[i]).astype(out.dtype)
            pltpu.make_async_copy(out, other_ref, out_sem.at[0]).start()
        else:
            keep[i] += got[i]
            pltpu.make_async_copy(keep.at[i], mine_ref, out_sem.at[1]).start()
    pltpu.make_async_copy(out, other_ref, out_sem.at[0]).wait()
    pltpu.make_async_copy(keep.at[1], mine_ref, out_sem.at[1]).wait()


def add_cores(keep, got):
    part = keep.shape[1:]
    return pl.pallas_call(
        add_cores_kernel,
        out_shape=[jax.ShapeDtypeStruct(part, jnp.float32), jax.ShapeDtypeStruct(part, jnp.bfloat16)],
        in_specs=[HBM, HBM],
        out_specs=[HBM, HBM],
        scratch_shapes=[
            pltpu.VMEM(keep.shape, jnp.float32),
            pltpu.VMEM(keep.shape, jnp.float32),
            pltpu.VMEM(part, jnp.bfloat16),
            pltpu.SemaphoreType.DMA((4,)),
            pltpu.SemaphoreType.DMA((2,)),
        ],
        compiler_params=pltpu.CompilerParams(vmem_limit_bytes=VMEM_GRANT),
        cost_estimate=LITTLE,
    )(keep, got)


def add_shares(share):
    return lax.psum_scatter(share, "tp", scatter_dimension=1, tiled=True).astype(jnp.bfloat16)


def body(
    cand_count,
    tp_count,
    reward_query,
    reward_new,
    reward_key_value_cache,
    reward_length,
    out_weight,
    policy_cache,
    policy_length,
    source,
    policy_query,
    policy_new,
):
    policy = spread_policy
    if (cand_count, tp_count, policy_cache.shape[0], source.shape[0]) == (GRID, 4, 8, SLOTS):
        policy = routed_policy
    reward_inputs = (reward_query, reward_new, reward_key_value_cache, reward_length, out_weight)
    return policy(policy_cache, policy_length, source, policy_query, policy_new, reward_inputs)


def solution(mesh):
    in_specs = (
        P("cand", None, "tp"),
        P("cand", None, None, "tp"),
        P("cand", None, None, "tp"),
        P("cand"),
        P("tp", None),
        P("cand", None, None, "tp"),
        P(),
        P(),
        P("cand", "tp"),
        P("cand", None, "tp"),
    )
    out_specs = (P("cand", "tp"), P("cand", None, None, "tp"), P("cand", "tp"))
    return jax.shard_map(
        functools.partial(body, mesh.shape["cand"], mesh.shape["tp"]),
        mesh=mesh,
        in_specs=in_specs,
        out_specs=out_specs,
        check_vma=False,
    )
```
